256 devices in a mesh: row: 8 (over z_lo, core), col: 32 (over z_hi, x, y).
Axes of the slice: x: 4, y: 4, z: 8 (z_hi: 2, z_lo: 4; z = z_hi * 4 + z_lo), core: 2. Of those that a mesh axis runs over, the one named last changes fastest.
Arguments:
- kernel_codes: bfloat16 [24576, 49152], P('row', 'col'), may hold values from -4 to 4, as said below
- tile_scales: float32 [768, 1536], P('row', 'col'), as said below
- kernel_diagonal: float32 [49152], P('col'), may hold values from 0.5 to 1.5
- noise_variance: float32 [49152], P('col'), may hold values from 1 to 3
- targets: float32 [8, 49152], P(None, 'col'), may hold values from -25 to 25
Outputs:
- solution: float32 [8, 49152], P(None, 'col')
- residual: float32 [8, 49152], P(None, 'col')
The draws below stay inside these ranges and needn't reach their ends.
Inputs may be any that keep to these rules, and one draw needn't show every extreme that they name: `kernel_codes`: in every slot (s, s), the entry at row i and column i of its first 768 columns is zero and unused. tile_scales lies between 0.15 / sqrt(49152) and 0.6 / sqrt(49152).
All inputs are finite; a program needn't handle non-finite values.
Results may differ from the reference program's by a relative error of at most 0.0098.
Values may be sent and summed in bfloat16 or wider, within the bound.
No kernel may reach another device: no remote copies, remote signals or barrier semaphores. Data moves between devices by JAX's collectives and lax.ppermute only.
A program may use at most 256 MiB of HBM per device.

```python
import math
import jax
import jax.numpy as jnp
from jax import lax

RHS = 8
QB = 32
ITERS = 2
POINTS = 49152
TILE = 1536
HALF = 768


def draw_kernel_codes(key, part):
    key = jax.random.fold_in(key, 11)
    samples = jax.random.truncated_normal(key, -4.0, 4.0, (POINTS // 2, POINTS), jnp.float32)
    rows = jnp.arange(POINTS // 2, dtype=jnp.int32)[:, None]
    cols = jnp.arange(POINTS, dtype=jnp.int32)[None, :]
    unused = (rows // HALF == cols // TILE) & (rows % HALF == cols % TILE)
    return jnp.where(unused, 0.0, samples).astype(jnp.bfloat16)


def draw_tile_scales(key, part):
    key = jax.random.fold_in(key, 12)
    exponent = jax.random.uniform(key, (POINTS // (2 * QB), POINTS // QB), jnp.float32)
    base_scale = 0.3 / math.sqrt(POINTS)
    return base_scale * jnp.power(4.0, exponent - 0.5)


def draw_targets(key, part):
    key = jax.random.fold_in(key, 13)
    first_key, second_key, third_key = jax.random.split(key, 3)
    values = jax.random.truncated_normal(first_key, -4.0, 4.0, (RHS, POINTS), jnp.float32)
    row_scale = jnp.power(10.0, jax.random.uniform(second_key, (RHS,), jnp.float32) - 1.0)
    rough_scale = jnp.power(10.0, jax.random.uniform(third_key, (POINTS,), jnp.float32) - 0.5)
    position = jnp.arange(POINTS, dtype=jnp.float32) / POINTS
    rising = jnp.power(3.0, position - 0.5)
    return values * row_scale[:, None] * (rough_scale * rising)[None, :]


def block_levels(own_key, dims, cuts, smallest, high):
    gain, own = 1.0, jax.random.fold_in(own_key, 6)
    for dim, parts in cuts:
        steps = jnp.exp(jax.random.uniform(jax.random.fold_in(own, dim), (parts,), jnp.float32, smallest / len(cuts), high / len(cuts)))
        gain = gain * jnp.repeat(steps, dims[dim] // parts).reshape([-1 if axis == dim else 1 for axis in range(len(dims))])
    return gain


def setup_inputs(seed: int = 0) -> dict:
    key_list = jax.random.split(jax.random.key(seed), 6)
    return {
        "kernel_codes": draw_kernel_codes(jax.random.fold_in(key_list[5], 71), 0),
        "tile_scales": draw_tile_scales(jax.random.fold_in(key_list[5], 71), 0),
        "kernel_diagonal": jnp.clip(0.5 + 1.0 * jax.random.uniform(key_list[2], (POINTS,), jnp.float32) ** block_levels(key_list[2], (POINTS,), ((0, 32),), -0.2, 0.2), 0.5, 1.5),
        "noise_variance": jnp.clip(1.0 + 2.0 * jax.random.uniform(key_list[3], (POINTS,), jnp.float32) ** block_levels(key_list[3], (POINTS,), ((0, 32),), -0.2, 0.2), 1.0, 3.0),
        "targets": draw_targets(jax.random.fold_in(key_list[5], 71), 0),
    }


def inner_grams(left, right):
    return jnp.dot(left, right.T, precision=lax.Precision.HIGHEST)

def solve_small(matrix, right_side):
    factor = jnp.linalg.cholesky(matrix)
    return jax.scipy.linalg.cho_solve((factor, True), right_side)

def dequantize_slab(codes_rows, scale_rows):
    row_count, col_count = codes_rows.shape
    expanded = codes_rows.astype(jnp.float32).reshape(row_count // QB, QB, col_count // QB, QB)
    expanded = expanded * scale_rows[:, None, :, None]
    return expanded.reshape(row_count, col_count).astype(jnp.bfloat16)

def unpack_tile(slot, diag_vals):
    mixed = slot[:, :HALF]
    upper = slot[:, HALF:]
    index = jnp.arange(HALF, dtype=jnp.int32)
    lower_mask = index[:, None] > index[None, :]
    upper_mask = index[:, None] < index[None, :]
    diagonal_mask = index[:, None] == index[None, :]
    zero = jnp.zeros((), slot.dtype)
    low = jnp.where(lower_mask, mixed, zero)
    high = jnp.where(upper_mask, mixed, zero)
    first_quarter = low + low.T + jnp.where(diagonal_mask, diag_vals[None, :HALF], zero)
    last_quarter = high + high.T + jnp.where(diagonal_mask, diag_vals[None, HALF:], zero)
    top = jnp.concatenate([first_quarter, upper], axis=1)
    bottom = jnp.concatenate([upper.T, last_quarter], axis=1)
    return jnp.concatenate([top, bottom], axis=0)

def reference(kernel_codes, tile_scales, kernel_diagonal, noise_variance, targets):
    tiles = POINTS // TILE
    diag_rounded = kernel_diagonal.astype(jnp.bfloat16)
    order = jnp.arange(tiles, dtype=jnp.int32)

    def apply_kernel(rounded):
        blocks = rounded.astype(jnp.float32).reshape(RHS, tiles, TILE)

        def visit(total, index):
            codes_rows = lax.dynamic_slice_in_dim(kernel_codes, (index * HALF).astype(jnp.int32), HALF, 0)
            scale_rows = lax.dynamic_slice_in_dim(tile_scales, (index * (HALF // QB)).astype(jnp.int32), HALF // QB, 0)
            slab = dequantize_slab(codes_rows, scale_rows).reshape(HALF, tiles, TILE)
            wide = slab.astype(jnp.float32)
            own = lax.dynamic_index_in_dim(blocks, index, 1, keepdims=False)
            later = (order > index)[None, :, None]
            earlier = (order < index)[None, :, None]
            forward = jnp.einsum('rh,hbp->rbp', own[:, :HALF], wide, precision=lax.Precision.HIGHEST)
            backward = jnp.einsum('rp,hbp->rbh', own, wide, precision=lax.Precision.HIGHEST)
            padding = jnp.zeros((RHS, tiles, TILE - HALF), jnp.float32)
            to_others = jnp.where(later, forward, 0.0) + jnp.where(earlier, jnp.concatenate([padding, backward], axis=2), 0.0)
            gathered_from = jnp.einsum('rbh,hbp->rp', jnp.where(earlier, blocks[:, :, HALF:], 0.0), wide, precision=lax.Precision.HIGHEST)
            mirrored = jnp.einsum('rbp,hbp->rh', jnp.where(later, blocks, 0.0), wide, precision=lax.Precision.HIGHEST)
            diag_slot = lax.dynamic_index_in_dim(slab, index, 1, keepdims=False)
            diag_vals = lax.dynamic_slice_in_dim(diag_rounded, (index * TILE).astype(jnp.int32), TILE, 0)
            square = unpack_tile(diag_slot, diag_vals).astype(jnp.float32)
            to_self = gathered_from + jnp.concatenate([mirrored, jnp.zeros((RHS, TILE - HALF), jnp.float32)], axis=1)
            to_self = to_self + jnp.dot(own, square, precision=lax.Precision.HIGHEST)
            hit = (order == index)[None, :, None]
            total = total + to_others + jnp.where(hit, to_self[:, None, :], 0.0)
            return (total, None)
        total, unused = lax.scan(visit, jnp.zeros((RHS, tiles, TILE), jnp.float32), order)
        return total.reshape(RHS, POINTS)
    solution = jnp.zeros_like(targets)
    residual = targets
    direction = targets
    res_gram = inner_grams(residual, residual)
    for iteration in range(ITERS):
        rounded = direction.astype(jnp.bfloat16)
        applied = apply_kernel(rounded) + noise_variance[None, :] * direction
        curvature = inner_grams(direction, applied)
        step_weights = solve_small(curvature, res_gram)
        solution = solution + jnp.dot(step_weights.T, direction, precision=lax.Precision.HIGHEST)
        residual = residual - jnp.dot(step_weights.T, applied, precision=lax.Precision.HIGHEST)
        if iteration + 1 < ITERS:
            next_gram = inner_grams(residual, residual)
            blend_weights = solve_small(res_gram, next_gram)
            direction = residual + jnp.dot(blend_weights.T, direction, precision=lax.Precision.HIGHEST)
            res_gram = next_gram
    return (solution, residual)
```

```python
import functools

import jax
import jax.numpy as jnp
from jax import lax
from jax.experimental import pallas as pl
from jax.experimental.pallas import tpu as pltpu
from jax.sharding import PartitionSpec as P

F32 = jnp.float32
BF16 = jnp.bfloat16
SHIFT = 3.0
VMEM_LIMIT = 56 * 1024 * 1024


def dequantize_slot(codes_ref, scales_ref, out_ref):
    block_rows, col_blocks = scales_ref.shape
    rows, cols = codes_ref.shape
    order = rows // block_rows
    lane_block = lax.broadcasted_iota(jnp.int32, (col_blocks, cols), 1) // (cols // col_blocks)
    own_block = lax.broadcasted_iota(jnp.int32, (col_blocks, cols), 0)
    spread = jnp.where(lane_block == own_block, 1.0, 0.0).astype(F32)
    wide = jnp.dot(
        scales_ref[...], spread, precision=lax.Precision.HIGHEST, preferred_element_type=F32
    )
    for block in range(block_rows):
        part = slice(block * order, (block + 1) * order)
        out_ref[part, :] = (codes_ref[part, :].astype(F32) * wide[block : block + 1, :]).astype(BF16)


def slot_products(slot, offset, slab_ref, rows_ref, own_ref, out_ref, total_ref):
    half, tile = slab_ref.shape
    nt = (((1,), (1,)), ((), ()))
    own = own_ref[...]
    lanes = pl.multiple_of(slot * tile, tile)
    seen = rows_ref[:, pl.ds(lanes, tile)]

    @pl.when(slot == 0)
    def _():
        total_ref[...] = jnp.zeros_like(total_ref)

    @pl.when(slot < offset)
    def _():
        slab = slab_ref[...]
        total_ref[...] += jnp.dot(seen[:, :half], slab, preferred_element_type=F32)
        second = lax.dot_general(own, slab, nt, preferred_element_type=F32)
        out_ref[:, pl.ds(lanes, half)] = second.astype(BF16)
        out_ref[:, pl.ds(lanes + half, half)] = jnp.zeros_like(second).astype(BF16)

    @pl.when(slot > offset)
    def _():
        slab = slab_ref[...]
        first = jnp.dot(own[:, half:], slab, preferred_element_type=F32)
        out_ref[:, pl.ds(lanes, tile)] = first.astype(BF16)
        total_ref[:, half:] += lax.dot_general(seen, slab, nt, preferred_element_type=F32)

    @pl.when(slot == offset)
    def _():
        mixed = slab_ref[:, :half]
        upper = slab_ref[:, half:]
        row = lax.broadcasted_iota(jnp.int32, (half, half), 0)
        col = lax.broadcasted_iota(jnp.int32, (half, half), 1)
        zero = jnp.zeros_like(mixed)
        low = jnp.where(row > col, mixed, zero)
        high = jnp.where(row < col, mixed, zero)
        head = own[:, :half]
        tail = own[:, half:]
        dot = functools.partial(jnp.dot, preferred_element_type=F32)
        dot_t = functools.partial(
            lax.dot_general, dimension_numbers=nt, preferred_element_type=F32
        )
        total_ref[:, :half] += dot(head, low) + dot_t(head, low) + dot_t(tail, upper)
        total_ref[:, half:] += dot(head, upper) + dot(tail, high) + dot_t(tail, high)
        out_ref[:, pl.ds(lanes, tile)] = jnp.zeros((own.shape[0], tile), BF16)

    @pl.when(slot == pl.num_programs(0) - 1)
    def _():
        out_ref[:, pl.ds(pl.num_programs(0) * tile, tile)] = total_ref[...].astype(BF16)


def first_kernel(offset_ref, codes_ref, scales_ref, rows_ref, own_ref, slab_ref, out_ref, total_ref):
    dequantize_slot(codes_ref, scales_ref, slab_ref)
    slot_products(
        pl.program_id(0), offset_ref[0], slab_ref, rows_ref, own_ref, out_ref, total_ref
    )


def second_kernel(offset_ref, slab_ref, rows_ref, own_ref, out_ref, gram_ref, total_ref):
    slot_products(
        pl.program_id(0), offset_ref[0], slab_ref, rows_ref, own_ref, out_ref, total_ref
    )

    @pl.when(pl.program_id(0) == pl.num_programs(0) - 1)
    def _():
        nt = (((1,), (1,)), ((), ()))
        split = rows_ref.shape[1]
        gram_ref[...] = lax.dot_general(
            out_ref[:, :split], rows_ref[...], nt, preferred_element_type=F32
        ) + lax.dot_general(out_ref[:, split:], own_ref[...], nt, preferred_element_type=F32)


def whole(shape):
    return pl.BlockSpec(shape, lambda slot: (0,) * len(shape))


def apply_first(offset, codes, scales, rows, own, slots):
    height, tile = codes.shape
    rhs = own.shape[0]
    half = height // slots
    block = pl.BlockSpec((half, tile), lambda slot: (slot, 0))
    scale_block = pl.BlockSpec((scales.shape[0] // slots, scales.shape[1]), lambda slot: (slot, 0))
    width = (slots + 1) * tile
    return pl.pallas_call(
        first_kernel,
        grid=(slots,),
        in_specs=[
            pl.BlockSpec(memory_space=pltpu.SMEM),
            block,
            scale_block,
            whole(rows.shape),
            whole(own.shape),
        ],
        out_specs=[block, whole((rhs, width))],
        out_shape=[
            jax.ShapeDtypeStruct(codes.shape, BF16),
            jax.ShapeDtypeStruct((rhs, width), BF16),
        ],
        scratch_shapes=[pltpu.VMEM((rhs, tile), F32)],
        compiler_params=pltpu.CompilerParams(vmem_limit_bytes=VMEM_LIMIT),
        name="first_product",
    )(offset, codes, scales, rows, own)


def apply_second(offset, slabs, rows, own, slots):
    height, tile = slabs.shape
    rhs = own.shape[0]
    half = height // slots
    width = (slots + 1) * tile
    return pl.pallas_call(
        second_kernel,
        grid=(slots,),
        in_specs=[
            pl.BlockSpec(memory_space=pltpu.SMEM),
            pl.BlockSpec((half, tile), lambda slot: (slot, 0)),
            whole(rows.shape),
            whole(own.shape),
        ],
        out_specs=[whole((rhs, width)), whole((rhs, rhs))],
        out_shape=[
            jax.ShapeDtypeStruct((rhs, width), BF16),
            jax.ShapeDtypeStruct((rhs, rhs), F32),
        ],
        scratch_shapes=[pltpu.VMEM((rhs, tile), F32)],
        compiler_params=pltpu.CompilerParams(vmem_limit_bytes=VMEM_LIMIT),
        name="second_product",
    )(offset, slabs, rows, own)


def times(left, right):
    total = left[:, 0:1] * right[0:1, :]
    for index in range(1, left.shape[1]):
        total = total + left[:, index : index + 1] * right[index : index + 1, :]
    return total


def inverses(matrices):
    size = matrices[0].shape[0]
    row = lax.broadcasted_iota(jnp.int32, (size, size), 0)
    col = lax.broadcasted_iota(jnp.int32, (size, size), 1)
    eye = jnp.where(row == col, 1.0, 0.0).astype(F32)
    work = [(matrix, eye) for matrix in matrices]
    for step in range(size):
        here = row == step
        following = []
        for left, right in work:
            scale = 1.0 / left[step : step + 1, step : step + 1]
            left_row = left[step : step + 1, :] * scale
            right_row = right[step : step + 1, :] * scale
            column = left[:, step : step + 1]
            following.append(
                (
                    jnp.where(here, left_row, left - column * left_row),
                    jnp.where(here, right_row, right - column * right_row),
                )
            )
        work = following
    return [right for left, right in work], eye


def final_kernel(gram_ref, base_ref, mid_ref, top_ref, solution_ref, residual_ref):
    rhs = base_ref.shape[0]
    gram = gram_ref[...]
    bb, yb, yy, wy = (gram[:, index * rhs : (index + 1) * rhs] for index in range(4))
    curvature = yb + SHIFT * bb
    (inverse_curvature, inverse_bb), eye = inverses([curvature, bb])
    step_t = times(bb, inverse_curvature)
    step = times(inverse_curvature, bb)
    a1, a1_t = eye - SHIFT * step_t, eye - SHIFT * step
    b1, b1_t = -step_t, -step

    def inner(a, a_t, b, b_t, first, cross, last):
        return times(times(a, first) + times(b, cross), a_t) + times(
            times(a, cross) + times(b, last), b_t
        )

    next_gram = inner(a1, a1_t, b1, b1_t, bb, yb, yy)
    a2 = a1 + times(next_gram, inverse_bb)
    a2_t = a1_t + times(inverse_bb, next_gram)
    curvature = inner(a2, a2_t, b1, b1_t, yb + SHIFT * bb, yy + SHIFT * yb, wy + SHIFT * yy)
    (inverse_curvature,), eye = inverses([curvature])
    last_t = times(next_gram, inverse_curvature)
    base, mid, top = base_ref[...], mid_ref[...], top_ref[...]
    from_mid = times(last_t, b1)
    from_base = times(last_t, a2)
    solution_ref[...] = times(step_t + from_base, base) + times(from_mid, mid)
    residual_ref[...] = (
        times(a1 - SHIFT * from_base, base)
        + times(b1 - from_base - SHIFT * from_mid, mid)
        - times(from_mid, top)
    )


def finish(gram, base, mid, top):
    shape = jax.ShapeDtypeStruct(base.shape, F32)
    return pl.pallas_call(final_kernel, out_shape=[shape, shape], name="small_solves")(
        gram, base, mid, top
    )


def split_three(values):
    first = lax.reduce_precision(values, 8, 7)
    rest = values - first
    second = lax.reduce_precision(rest, 8, 7)
    return jnp.concatenate([first, second, rest - second], axis=-1).astype(BF16)


def join_three(parts):
    wide = parts.astype(F32)
    size = wide.shape[-1] // 3
    return wide[..., :size] + (wide[..., size : 2 * size] + wide[..., 2 * size :])


def local(kernel_codes, tile_scales, kernel_diagonal, noise_variance, targets):
    rhs, tile = targets.shape
    half = tile // 2
    slots = kernel_codes.shape[0] // half
    row_index = lax.axis_index("row")
    col_index = lax.axis_index("col")
    row_count = lax.axis_size("row")
    col_count = lax.axis_size("col")
    offset = (col_index - row_index * slots).astype(jnp.int32).reshape(1)
    own_tile = (jnp.arange(col_count) == col_index)[:, None]
    shifted = lax.reduce_precision(kernel_diagonal, 8, 7) + (noise_variance - SHIFT)
    base_row = lax.dynamic_index_in_dim(targets, row_index, 0, keepdims=False)

    def exchange(values, axis):
        return lax.all_to_all(values, axis, 0, 0)

    def everywhere(values):
        return exchange(jnp.broadcast_to(values[None], (col_count,) + values.shape), "col")

    def tile_sums(received):
        rows = received[:, : slots * tile].astype(F32).reshape(col_count, tile)
        own = jnp.sum(received[:, slots * tile : (slots + 1) * tile].astype(F32), axis=0)
        return (rows + jnp.where(own_tile, own[None, :], 0.0)).astype(BF16)

    spread = everywhere(base_row.astype(BF16)).reshape(row_count, slots * tile)
    rows = exchange(spread, "row")
    slabs, sums = apply_first(
        offset, kernel_codes, tile_scales, rows, targets.astype(BF16), slots
    )
    sums = exchange(tile_sums(exchange(sums, "row")), "col")
    mid_row = jnp.sum(sums.astype(F32), axis=0) + shifted * base_row
    mid_high = lax.reduce_precision(mid_row, 8, 7)
    mid_low = (mid_row - mid_high).astype(BF16)
    mid_high = mid_high.astype(BF16)
    spread = everywhere(mid_high).reshape(row_count, slots * tile)
    own_pair = jnp.concatenate([mid_high, mid_low])
    spread = jnp.concatenate(
        [spread, jnp.broadcast_to(own_pair[None], (row_count, 2 * tile))], axis=1
    )
    rows = exchange(spread, "row")
    own_high = rows[:, slots * tile : (slots + 1) * tile]
    mid = own_high.astype(F32) + rows[:, (slots + 1) * tile :].astype(F32)
    sums, gram = apply_second(offset, slabs, rows[:, : slots * tile], own_high, slots)
    gram = jnp.pad(split_three(gram), ((0, 0), (0, 128 - 3 * rhs)))
    received = exchange(jnp.concatenate([sums, gram], axis=1), "row")
    gram_row = join_three(
        jnp.sum(received[:, (slots + 1) * tile :][:, : 3 * rhs].astype(F32), axis=0)
    )
    local_grams = jnp.dot(
        jnp.stack([base_row, mid_row, shifted * mid_row]),
        jnp.concatenate([targets, mid], axis=0).T,
        precision=lax.Precision.HIGHEST,
    )
    grams = jnp.concatenate(
        [
            local_grams[0, :rhs],
            local_grams[1, :rhs],
            local_grams[1, rhs:],
            local_grams[2, rhs:] + gram_row,
        ]
    )
    grams = jnp.pad(split_three(grams), (0, 128 - 12 * rhs))
    outgoing = jnp.concatenate(
        [tile_sums(received), jnp.broadcast_to(grams[None], (col_count, 128))], axis=1
    )
    sums = jnp.sum(exchange(outgoing, "col").astype(F32), axis=0)
    top_row = sums[:tile] + shifted * mid_row
    grams = jnp.pad(join_three(sums[tile : tile + 12 * rhs]), (0, 128 - 4 * rhs))
    last = exchange(
        jnp.broadcast_to(jnp.concatenate([top_row, grams])[None], (row_count, tile + 128)), "row"
    )
    return tuple(finish(last[:, tile : tile + 4 * rhs], targets, mid, last[:, :tile]))


def solution(mesh):
    in_specs = (P("row", "col"), P("row", "col"), P("col"), P("col"), P(None, "col"))
    out_specs = (P(None, "col"), P(None, "col"))
    return jax.shard_map(local, mesh=mesh, in_specs=in_specs, out_specs=out_specs, check_vma=False)
```

```python
import jax
import jax.numpy as jnp
from jax import lax
from jax.experimental import pallas as pl
from jax.experimental.pallas import tpu as pltpu
from jax.sharding import PartitionSpec as P

F32 = jnp.float32
BF16 = jnp.bfloat16
SHIFT = 3.0
VMEM_LIMIT = 56 * 1024 * 1024


def dequantize_slot(codes_ref, scales_ref, out_ref):
    block_rows, col_blocks = scales_ref.shape
    rows, cols = codes_ref.shape
    order = rows // block_rows
    lane_block = lax.broadcasted_iota(jnp.int32, (col_blocks, cols), 1) // (cols // col_blocks)
    own_block = lax.broadcasted_iota(jnp.int32, (col_blocks, cols), 0)
    spread = jnp.where(lane_block == own_block, 1.0, 0.0).astype(F32)
    wide = jnp.dot(
        scales_ref[...], spread, precision=lax.Precision.HIGHEST, preferred_element_type=F32
    )
    for block in range(block_rows):
        part = slice(block * order, (block + 1) * order)
        out_ref[part, :] = (codes_ref[part, :].astype(F32) * wide[block : block + 1, :]).astype(BF16)


NT = (((1,), (1,)), ((), ()))


def dot(left, right):
    return jnp.dot(left, right, preferred_element_type=F32)


def dot_t(left, right):
    return lax.dot_general(left, right, NT, preferred_element_type=F32)


def triangles(slab_ref):
    half = slab_ref.shape[0]
    mixed = slab_ref[:, :half]
    row = lax.broadcasted_iota(jnp.int32, (half, half), 0)
    col = lax.broadcasted_iota(jnp.int32, (half, half), 1)
    zero = jnp.zeros_like(mixed)
    return jnp.where(row > col, mixed, zero), jnp.where(row < col, mixed, zero)


def toward_rows(slot, place_ref, slab_ref, own_ref, out_ref, extra_ref):
    half, tile = slab_ref.shape
    rhs = own_ref.shape[0]
    offset = place_ref[0]
    own = own_ref[...]
    row = lax.broadcasted_iota(jnp.int32, (rhs, tile), 0)
    share = jnp.sum(jnp.where(row == place_ref[1], own.astype(F32), 0.0), axis=0, keepdims=True)
    out_ref[0, :, tile:] = jnp.broadcast_to(share, (rhs, tile)).astype(BF16)

    @pl.when(slot == 0)
    def _():
        extra_ref[...] = jnp.zeros_like(extra_ref)

    @pl.when(slot < offset)
    def _():
        second = dot_t(own, slab_ref[...])
        out_ref[0, :, :half] = second.astype(BF16)
        out_ref[0, :, half:tile] = jnp.zeros((rhs, tile - half), BF16)

    @pl.when(slot > offset)
    def _():
        out_ref[0, :, :tile] = dot(own[:, half:], slab_ref[...]).astype(BF16)

    @pl.when(slot == offset)
    def _():
        low, high = triangles(slab_ref)
        head, tail = own[:, :half], own[:, half:]
        extra_ref[:, :half] = dot_t(head, low) + dot_t(tail, slab_ref[:, half:])
        extra_ref[:, half:] = dot_t(tail, high)
        out_ref[0, :, :tile] = jnp.zeros((rhs, tile), BF16)


def first_rows_kernel(place_ref, codes_ref, scales_ref, own_ref, slab_ref, out_ref, extra_ref):
    dequantize_slot(codes_ref, scales_ref, slab_ref)
    toward_rows(pl.program_id(0), place_ref, slab_ref, own_ref, out_ref, extra_ref)


def combine(received_ref, base, shifted):
    rhs, tile = base.shape
    rows = [
        jnp.sum(received_ref[:, part * tile : (part + 1) * tile].astype(F32), axis=0, keepdims=True)
        for part in range(rhs)
    ]
    others = received_ref[:, rhs * tile : (rhs + 1) * tile].astype(F32)
    return (jnp.concatenate(rows, axis=0) + others) + shifted * base


def second_rows_kernel(
    place_ref, slab_ref, received_ref, base_ref, shifted_ref, out_ref, extra_ref, mid_ref, own_ref
):
    @pl.when(pl.program_id(0) == 0)
    def _():
        mid = combine(received_ref, base_ref[...], shifted_ref[...])
        mid_ref[...] = mid
        own_ref[...] = mid.astype(BF16)

    toward_rows(pl.program_id(0), place_ref, slab_ref, own_ref, out_ref, extra_ref)


def toward_own_kernel(
    place_ref, slab_ref, rows_ref, own_ref, extra_ref, reduced_ref, out_ref, total_ref
):
    half, tile = slab_ref.shape
    rhs = own_ref.shape[0]
    slot = pl.program_id(0)
    offset = place_ref[0]
    lanes = pl.multiple_of(slot * tile, tile)

    @pl.when(slot == 0)
    def _():
        total_ref[...] = extra_ref[...]

    @pl.when(slot < offset)
    def _():
        total_ref[...] += dot(rows_ref[:, pl.ds(lanes, half)], slab_ref[...])

    @pl.when(slot > offset)
    def _():
        total_ref[:, half:] += dot_t(rows_ref[:, pl.ds(lanes, tile)], slab_ref[...])

    @pl.when(slot == offset)
    def _():
        low, high = triangles(slab_ref)
        own = own_ref[...]
        head, tail = own[:, :half], own[:, half:]
        total_ref[:, :half] += dot(head, low)
        total_ref[:, half:] += dot(head, slab_ref[:, half:]) + dot(tail, high)

    @pl.when(slot == pl.num_programs(0) - 1)
    def _():
        for part in range(rhs):
            out_ref[:, part * tile : (part + 1) * tile] = jnp.broadcast_to(
                total_ref[part : part + 1, :], (out_ref.shape[0], tile)
            ).astype(BF16)
        out_ref[:, rhs * tile :] = jnp.broadcast_to(
            reduced_ref[...], (out_ref.shape[0], tile)
        ).astype(BF16)


def whole(shape):
    return pl.BlockSpec(shape, lambda slot: (0,) * len(shape))


SMEM = pl.BlockSpec(memory_space=pltpu.SMEM)
PARAMS = pltpu.CompilerParams(vmem_limit_bytes=VMEM_LIMIT)


def block_specs(codes, rhs, slots):
    height, tile = codes.shape
    return (
        pl.BlockSpec((height // slots, tile), lambda slot: (slot, 0)),
        pl.BlockSpec((1, rhs, 2 * tile), lambda slot: (slot, 0, 0)),
    )


def first_rows(place, codes, scales, own, slots):
    rhs, tile = own.shape
    block, out_block = block_specs(codes, rhs, slots)
    scale_block = pl.BlockSpec((scales.shape[0] // slots, scales.shape[1]), lambda slot: (slot, 0))
    return pl.pallas_call(
        first_rows_kernel,
        grid=(slots,),
        in_specs=[SMEM, block, scale_block, whole(own.shape)],
        out_specs=[block, out_block, whole((rhs, tile))],
        out_shape=[
            jax.ShapeDtypeStruct(codes.shape, BF16),
            jax.ShapeDtypeStruct((slots, rhs, 2 * tile), BF16),
            jax.ShapeDtypeStruct((rhs, tile), F32),
        ],
        compiler_params=PARAMS,
        name="first_rows",
    )(place, codes, scales, own)


def second_rows(place, slabs, received, base, shifted, slots):
    rhs, tile = base.shape
    block, out_block = block_specs(slabs, rhs, slots)
    return pl.pallas_call(
        second_rows_kernel,
        grid=(slots,),
        in_specs=[SMEM, block, whole(received.shape), whole(base.shape), whole(shifted.shape)],
        out_specs=[out_block] + [whole((rhs, tile))] * 3,
        out_shape=[
            jax.ShapeDtypeStruct((slots, rhs, 2 * tile), BF16),
            jax.ShapeDtypeStruct((rhs, tile), F32),
            jax.ShapeDtypeStruct((rhs, tile), F32),
            jax.ShapeDtypeStruct((rhs, tile), BF16),
        ],
        compiler_params=PARAMS,
        name="second_rows",
    )(place, slabs, received, base, shifted)


def toward_own(place, slabs, rows, own, extra, reduced, slots, copies):
    rhs, tile = own.shape
    block, unused = block_specs(slabs, rhs, slots)
    width = (rhs + 1) * tile
    return pl.pallas_call(
        toward_own_kernel,
        grid=(slots,),
        in_specs=[
            SMEM,
            block,
            whole(rows.shape),
            whole(own.shape),
            whole(extra.shape),
            whole(reduced.shape),
        ],
        out_specs=whole((copies, width)),
        out_shape=jax.ShapeDtypeStruct((copies, width), BF16),
        scratch_shapes=[pltpu.VMEM((rhs, tile), F32)],
        compiler_params=PARAMS,
        name="toward_own",
    )(place, slabs, rows, own, extra, reduced)


def times(left, right):
    total = left[:, 0:1] * right[0:1, :]
    for index in range(1, left.shape[1]):
        total = total + left[:, index : index + 1] * right[index : index + 1, :]
    return total


def inverses(matrices):
    size = matrices[0].shape[0]
    row = lax.broadcasted_iota(jnp.int32, (size, size), 0)
    col = lax.broadcasted_iota(jnp.int32, (size, size), 1)
    eye = jnp.where(row == col, 1.0, 0.0).astype(F32)
    work = [(matrix, eye) for matrix in matrices]
    for step in range(size):
        here = row == step
        following = []
        for left, right in work:
            scale = 1.0 / left[step : step + 1, step : step + 1]
            left_row = left[step : step + 1, :] * scale
            right_row = right[step : step + 1, :] * scale
            column = left[:, step : step + 1]
            following.append(
                (
                    jnp.where(here, left_row, left - column * left_row),
                    jnp.where(here, right_row, right - column * right_row),
                )
            )
        work = following
    return [right for left, right in work], eye


def final_kernel(
    gram_ref, received_ref, base_ref, mid_ref, shifted_ref, solution_ref, residual_ref
):
    rhs = base_ref.shape[0]
    gram = gram_ref[...]
    half_wy, bb, yb, yy, wy = (gram[:, index * rhs : (index + 1) * rhs] for index in range(5))
    wy = wy + (half_wy + half_wy.T)
    curvature = yb + SHIFT * bb
    (inverse_curvature, inverse_bb), eye = inverses([curvature, bb])
    step_t = times(bb, inverse_curvature)
    step = times(inverse_curvature, bb)
    a1, a1_t = eye - SHIFT * step_t, eye - SHIFT * step
    b1, b1_t = -step_t, -step

    def inner(a, a_t, b, b_t, first, cross, last):
        return times(times(a, first) + times(b, cross), a_t) + times(
            times(a, cross) + times(b, last), b_t
        )

    next_gram = inner(a1, a1_t, b1, b1_t, bb, yb, yy)
    a2 = a1 + times(next_gram, inverse_bb)
    a2_t = a1_t + times(inverse_bb, next_gram)
    curvature = inner(a2, a2_t, b1, b1_t, yb + SHIFT * bb, yy + SHIFT * yb, wy + SHIFT * yy)
    (inverse_curvature,), eye = inverses([curvature])
    last_t = times(next_gram, inverse_curvature)
    base, mid = base_ref[...], mid_ref[...]
    top = combine(received_ref, mid, shifted_ref[...])
    from_mid = times(last_t, b1)
    from_base = times(last_t, a2)
    solution_ref[...] = times(step_t + from_base, base) + times(from_mid, mid)
    residual_ref[...] = (
        times(a1 - SHIFT * from_base, base)
        + times(b1 - from_base - SHIFT * from_mid, mid)
        - times(from_mid, top)
    )


def finish(gram, received, base, mid, shifted):
    shape = jax.ShapeDtypeStruct(base.shape, F32)
    return pl.pallas_call(
        final_kernel, out_shape=[shape, shape], compiler_params=PARAMS, name="small_solves"
    )(gram, received, base, mid, shifted)


def split_three(values):
    first = lax.reduce_precision(values, 8, 7)
    rest = values - first
    second = lax.reduce_precision(rest, 8, 7)
    return jnp.concatenate([first, second, rest - second], axis=-1).astype(BF16)


def join_three(parts):
    wide = parts.astype(F32)
    size = wide.shape[-1] // 3
    return wide[..., :size] + (wide[..., size : 2 * size] + wide[..., 2 * size :])


def local(kernel_codes, tile_scales, kernel_diagonal, noise_variance, targets):
    rhs, tile = targets.shape
    slots = kernel_codes.shape[0] // (tile // 2)
    row_index = lax.axis_index("row")
    col_index = lax.axis_index("col")
    row_count = lax.axis_size("row")
    col_count = lax.axis_size("col")
    place = jnp.stack([col_index - row_index * slots, row_index]).astype(jnp.int32)
    shifted = lax.reduce_precision(kernel_diagonal, 8, 7) + (noise_variance - SHIFT)
    moves = [
        (row * col_count + col, (col % rhs) * col_count + slots * row + col // rhs)
        for row in range(row_count)
        for col in range(col_count)
    ]

    def exchange(values, axis):
        return lax.all_to_all(values, axis, 0, 0)

    def bring(outgoing):
        received = exchange(outgoing.reshape(col_count, 2 * tile), "col")
        reduced = jnp.sum(received[:, :tile].astype(F32), axis=0, keepdims=True)
        reduced = lax.ppermute(reduced, ("row", "col"), moves)
        rows = exchange(received[:, tile:].reshape(row_count, slots * tile), "row")
        return rows, reduced

    def pick(values):
        return lax.dynamic_index_in_dim(values, row_index, 0, keepdims=True)

    own = targets.astype(BF16)
    slabs, outgoing, extra = first_rows(place, kernel_codes, tile_scales, own, slots)
    rows, reduced = bring(outgoing)
    message = toward_own(place, slabs, rows, own, extra, reduced, slots, row_count)
    received = exchange(message, "row")
    outgoing, extra, mid, own = second_rows(
        place, slabs, received, targets, shifted[None, :], slots
    )
    rows, reduced = bring(outgoing)
    mid_row = pick(mid)
    grams = jnp.dot(
        jnp.concatenate([reduced, pick(targets), mid_row, shifted[None, :] * mid_row]),
        jnp.concatenate([targets, mid]).T,
        precision=lax.Precision.HIGHEST,
    )
    grams = jnp.concatenate(
        [grams[0, rhs:], grams[1, :rhs], grams[2, :rhs], grams[2, rhs:], grams[3, rhs:]]
    )
    grams = jnp.pad(grams, (0, 128 - 5 * rhs))
    grams = exchange(jnp.broadcast_to(grams[None], (col_count, 128)), "col")
    grams = jnp.pad(split_three(jnp.sum(grams, axis=0)[: 5 * rhs]), (0, 128 - 15 * rhs))
    message = toward_own(place, slabs, rows, own, extra, reduced, slots, row_count)
    message = jnp.concatenate(
        [message, jnp.broadcast_to(grams[None], (row_count, 128))], axis=1
    )
    received = exchange(message, "row")
    grams = join_three(received[:, (rhs + 1) * tile :][:, : 15 * rhs])
    return tuple(finish(grams, received, targets, mid, shifted[None, :]))


def solution(mesh):
    in_specs = (P("row", "col"), P("row", "col"), P("col"), P("col"), P(None, "col"))
    out_specs = (P(None, "col"), P(None, "col"))
    return jax.shard_map(local, mesh=mesh, in_specs=in_specs, out_specs=out_specs, check_vma=False)
```

```python
import functools

import jax
import jax.numpy as jnp
from jax import lax
from jax.experimental import pallas as pl
from jax.experimental.pallas import tpu as pltpu
from jax.sharding import PartitionSpec as P

F32 = jnp.float32
BF16 = jnp.bfloat16
SHIFT = 3.0
VMEM_LIMIT = 56 * 1024 * 1024


def dequantize_slot(codes_ref, scales_ref, out_ref):
    block_rows, col_blocks = scales_ref.shape
    rows, cols = codes_ref.shape
    order = rows // block_rows
    lane_block = lax.broadcasted_iota(jnp.int32, (col_blocks, cols), 1) // (cols // col_blocks)
    own_block = lax.broadcasted_iota(jnp.int32, (col_blocks, cols), 0)
    spread = jnp.where(lane_block == own_block, 1.0, 0.0).astype(F32)
    wide = jnp.dot(
        scales_ref[...], spread, precision=lax.Precision.HIGHEST, preferred_element_type=F32
    )
    for block in range(block_rows):
        part = slice(block * order, (block + 1) * order)
        out_ref[part, :] = (codes_ref[part, :].astype(F32) * wide[block : block + 1, :]).astype(BF16)


NT = (((1,), (1,)), ((), ()))


def dot(left, right):
    return jnp.dot(left, right, preferred_element_type=F32)


def dot_t(left, right):
    return lax.dot_general(left, right, NT, preferred_element_type=F32)


def triangles(slab_ref):
    half = slab_ref.shape[0]
    mixed = slab_ref[:, :half]
    row = lax.broadcasted_iota(jnp.int32, (half, half), 0)
    col = lax.broadcasted_iota(jnp.int32, (half, half), 1)
    zero = jnp.zeros_like(mixed)
    return jnp.where(row > col, mixed, zero), jnp.where(row < col, mixed, zero)


LANES = 128


def to_tiles(values):
    count = values.shape[1] // LANES
    return jnp.concatenate(
        [values[:, part * LANES : (part + 1) * LANES] for part in range(count)], axis=0
    )


def from_tiles(tiles, rhs):
    count = tiles.shape[0] // rhs
    return jnp.concatenate(
        [tiles[part * rhs : (part + 1) * rhs, :] for part in range(count)], axis=1
    )


def row_tiles(values):
    return values.reshape(values.shape[0], values.shape[1] // LANES, LANES)


def flat_rows(tiles):
    return tiles.reshape(tiles.shape[0], tiles.shape[1] * LANES)


def share_of(values, row_index):
    tiles = row_tiles(values)
    row = lax.broadcasted_iota(jnp.int32, tiles.shape, 0)
    return jnp.sum(jnp.where(row == row_index, tiles, 0.0), axis=0)


def toward_rows(slot, offset, slab_ref, own, put, extra_ref):
    half, tile = slab_ref.shape
    rhs = own.shape[0]

    @pl.when(slot == 0)
    def _():
        extra_ref[...] = jnp.zeros_like(extra_ref)

    @pl.when(slot < offset)
    def _():
        second = dot_t(own, slab_ref[...])
        put(jnp.concatenate([second, jnp.zeros((rhs, tile - half), F32)], axis=1))

    @pl.when(slot > offset)
    def _():
        put(dot(own[:, half:], slab_ref[...]))

    @pl.when(slot == offset)
    def _():
        low, high = triangles(slab_ref)
        head, tail = own[:, :half], own[:, half:]
        extra_ref[:, :half] = dot_t(head, low) + dot_t(tail, slab_ref[:, half:])
        extra_ref[:, half:] = dot_t(tail, high)
        put(jnp.zeros((rhs, tile), F32))


def first_rows_kernel(place_ref, codes_ref, scales_ref, base_ref, slab_ref, out_ref, extra_ref):
    dequantize_slot(codes_ref, scales_ref, slab_ref)
    rhs, tile = base_ref.shape
    size = rhs * tile // LANES
    base = base_ref[...]
    share = share_of(base, place_ref[1]).astype(BF16)
    for copy in range(out_ref.shape[0]):
        out_ref[copy, 0, size:, :] = share

    def put(values):
        tiles = to_tiles(values).astype(BF16)
        for copy in range(out_ref.shape[0]):
            out_ref[copy, 0, :size, :] = tiles

    toward_rows(pl.program_id(0), place_ref[0], slab_ref, base.astype(BF16), put, extra_ref)


def second_rows_kernel(place_ref, slab_ref, own_ref, out_ref, extra_ref):
    def put(values):
        out_ref[0, :, :] = values.astype(BF16)

    toward_rows(pl.program_id(0), place_ref[0], slab_ref, own_ref[...], put, extra_ref)


def relay_kernel(received_ref, out_ref):
    senders, height, lanes = received_ref.shape
    copies, parts, width, lanes = out_ref.shape
    size = height - width
    slots = parts - 1
    rhs = size // width
    reduced = received_ref[0, :size, :].astype(F32)
    for sender in range(1, senders):
        reduced = reduced + received_ref[sender, :size, :].astype(F32)
    rows = row_tiles(from_tiles(reduced, rhs)).astype(BF16)
    for copy in range(copies):
        first = (copy % (senders // slots)) * slots
        out_ref[copy, :slots, :, :] = received_ref[first : first + slots, size:, :]
        out_ref[copy, slots, :, :] = rows[copy % rhs]


def gather_rows(place_ref, received_ref, rows_ref, tile, slots):
    rhs = rows_ref.shape[0]
    start = place_ref[5] * rhs
    for part in range(slots):
        piece = received_ref[pl.ds(start, rhs), part, :, :].astype(F32)
        rows_ref[:, part * tile : (part + 1) * tile] = flat_rows(piece).astype(BF16)


def toward_own(slot, offset, slab_ref, rows_ref, own, total_ref):
    half, tile = slab_ref.shape
    lanes = pl.multiple_of(slot * tile, tile)

    @pl.when(slot < offset)
    def _():
        total_ref[...] += dot(rows_ref[:, pl.ds(lanes, half)], slab_ref[...])

    @pl.when(slot > offset)
    def _():
        total_ref[:, half:] += dot_t(rows_ref[:, pl.ds(lanes, tile)], slab_ref[...])

    @pl.when(slot == offset)
    def _():
        low, high = triangles(slab_ref)
        head, tail = own[:, :half], own[:, half:]
        total_ref[:, :half] += dot(head, low)
        total_ref[:, half:] += dot(head, slab_ref[:, half:]) + dot(tail, high)


def first_own_kernel(
    place_ref, slab_ref, received_ref, base_ref, extra_ref, out_ref, total_ref, rows_ref
):
    slot, slots = pl.program_id(0), rows_ref.shape[1] // base_ref.shape[1]
    rhs, tile = base_ref.shape

    @pl.when(slot == 0)
    def _():
        total_ref[...] = extra_ref[...]
        gather_rows(place_ref, received_ref, rows_ref, tile, slots)

    toward_own(slot, place_ref[0], slab_ref, rows_ref, base_ref[...].astype(BF16), total_ref)

    @pl.when(slot == slots - 1)
    def _():
        size = rhs * tile // LANES
        source = place_ref[6]
        planes = received_ref.shape[0] // rhs
        reduced = received_ref[source, slots, :, :].astype(F32)
        for plane in range(1, planes):
            reduced = reduced + received_ref[plane * rhs + source, slots, :, :].astype(F32)
        reduced = reduced.astype(BF16)
        tiles = to_tiles(total_ref[...]).astype(BF16)
        for copy in range(out_ref.shape[0]):
            out_ref[copy, :size, :] = tiles
            out_ref[copy, size:, :] = reduced


def combine_kernel(place_ref, received_ref, base_ref, shifted_ref, mid_ref, own_ref, out_ref):
    rhs, tile = base_ref.shape
    size = rhs * tile // LANES
    total = received_ref[0, :size, :].astype(F32)
    for sender in range(1, received_ref.shape[0]):
        total = total + received_ref[sender, :size, :].astype(F32)
    others = flat_rows(received_ref[:, size:, :].astype(F32))
    mid = (from_tiles(total, rhs) + others) + shifted_ref[...] * base_ref[...]
    mid_ref[...] = mid
    own_ref[...] = mid.astype(BF16)
    share = share_of(mid, place_ref[1]).astype(BF16)
    for copy in range(out_ref.shape[0]):
        out_ref[copy, :, :] = share


def three_parts(values):
    first = values.astype(BF16).astype(F32)
    rest = values - first
    second = rest.astype(BF16).astype(F32)
    return first, second, rest - second


def second_own_kernel(
    place_ref, slab_ref, received_ref, own_ref, extra_ref, sent_ref, grams_ref,
    out_ref, total_ref, rows_ref, sums_ref,
):
    slot = pl.program_id(0)
    rhs, tile = own_ref.shape
    slots = rows_ref.shape[1] // tile

    @pl.when(slot == 0)
    def _():
        total_ref[...] = extra_ref[...]
        gather_rows(place_ref, received_ref, rows_ref, tile, slots)

    toward_own(slot, place_ref[0], slab_ref, rows_ref, own_ref[...], total_ref)

    @pl.when(slot == slots - 1)
    def _():
        blank = jnp.zeros((rhs, out_ref.shape[2] * LANES - tile), F32)
        pair = dot_t(extra_ref[...].astype(BF16), own_ref[...])
        for part in range(slots):
            pair = pair + dot_t(sent_ref[part], rows_ref[:, part * tile : (part + 1) * tile])
            piece = jnp.concatenate([sent_ref[part].astype(F32), blank], axis=1)
            piece = row_tiles(piece).astype(BF16)
            for first in range(0, out_ref.shape[0], rhs):
                out_ref[first : first + rhs, part, :, :] = piece
        sums_ref[...] = grams_ref[...]
        sums_ref[:, :rhs] = pair
        pieces = [total_ref[...], *three_parts(sums_ref[...])]
        pieces.append(blank[:, (len(pieces) - 1) * LANES :])
        piece = row_tiles(jnp.concatenate(pieces, axis=1)).astype(BF16)
        for first in range(0, out_ref.shape[0], rhs):
            out_ref[first : first + rhs, slots, :, :] = piece


def joined(values, width):
    return (values[width : width + 1] + values[width + 1 : width + 2]) + values[width + 2 : width + 3]


def reduce_kernel(width, place_ref, received_ref, out_ref):
    senders, parts, height, lanes = received_ref.shape
    slots = parts - 1
    plane, own_place = place_ref[2], place_ref[4]
    count = out_ref.shape[0]
    planes = count // (slots * slots) * 2
    rhs = senders // planes
    row = lax.broadcasted_iota(jnp.int32, (height, lanes), 0)

    def take(sender, part):
        return received_ref[sender, part, :, :].astype(F32)

    own = take(plane * rhs, slots)
    rest = take((planes - 1 - plane) * rhs, slots)
    for sender in range(1, rhs):
        own = own + take(plane * rhs + sender, slots)
        rest = rest + take((planes - 1 - plane) * rhs + sender, slots)
    first, second, third = three_parts(joined(own + rest, width))
    grams = jnp.where(
        row == width, first, jnp.where(row == width + 1, second, jnp.where(row == width + 2, third, 0.0))
    )
    for target in range(count):
        sender = plane * (rhs // planes) + target // slots
        value = take(sender, target % slots) + take(rhs + sender, target % slots)
        value = value + jnp.where(own_place == target, own, 0.0)
        out_ref[target, :, :] = jnp.where(row < width, value, grams).astype(BF16)


def finish_reduce_kernel(width, received_ref, out_ref):
    total = received_ref[0, :, :].astype(F32)
    for sender in range(1, received_ref.shape[0]):
        total = total + received_ref[sender, :, :].astype(F32)
    row = lax.broadcasted_iota(jnp.int32, total.shape, 0)
    value = jnp.where(row < width, total, jnp.broadcast_to(joined(total, width), total.shape))
    for copy in range(out_ref.shape[0]):
        out_ref[copy, :, :] = value


def whole(shape):
    return pl.BlockSpec(shape, lambda slot: (0,) * len(shape))


SMEM = pl.BlockSpec(memory_space=pltpu.SMEM)
PARAMS = pltpu.CompilerParams(vmem_limit_bytes=VMEM_LIMIT)


def struct(shape, dtype):
    return jax.ShapeDtypeStruct(shape, dtype)


def plain(kernel, outs, name, *operands, scalars=True):
    specs = [pl.BlockSpec(memory_space=pltpu.VMEM)] * len(operands)
    if scalars:
        specs[0] = SMEM
    return pl.pallas_call(
        kernel, in_specs=specs, out_shape=outs, compiler_params=PARAMS, name=name
    )(*operands)


def slab_spec(codes, slots):
    return pl.BlockSpec((codes.shape[0] // slots, codes.shape[1]), lambda slot: (slot, 0))


def times(left, right):
    total = left[:, 0:1] * right[0:1, :]
    for index in range(1, left.shape[1]):
        total = total + left[:, index : index + 1] * right[index : index + 1, :]
    return total


def inverses(matrices):
    size = matrices[0].shape[0]
    row = lax.broadcasted_iota(jnp.int32, (size, size), 0)
    col = lax.broadcasted_iota(jnp.int32, (size, size), 1)
    eye = jnp.where(row == col, 1.0, 0.0).astype(F32)
    work = [(matrix, eye) for matrix in matrices]
    for step in range(size):
        here = row == step
        following = []
        for left, right in work:
            scale = 1.0 / left[step : step + 1, step : step + 1]
            left_row = left[step : step + 1, :] * scale
            right_row = right[step : step + 1, :] * scale
            column = left[:, step : step + 1]
            following.append(
                (
                    jnp.where(here, left_row, left - column * left_row),
                    jnp.where(here, right_row, right - column * right_row),
                )
            )
        work = following
    return [right for left, right in work], eye


def final_kernel(
    received_ref, base_ref, mid_ref, shifted_ref, solution_ref, residual_ref
):
    rhs, tile = base_ref.shape
    received = flat_rows(received_ref[...])
    gram = received[:, tile : tile + LANES]
    half_wy, bb, yb, yy, wy = (gram[:, index * rhs : (index + 1) * rhs] for index in range(5))
    wy = wy + (half_wy + half_wy.T)
    curvature = yb + SHIFT * bb
    (inverse_curvature, inverse_bb), eye = inverses([curvature, bb])
    step_t = times(bb, inverse_curvature)
    step = times(inverse_curvature, bb)
    a1, a1_t = eye - SHIFT * step_t, eye - SHIFT * step
    b1, b1_t = -step_t, -step

    def inner(a, a_t, b, b_t, first, cross, last):
        return times(times(a, first) + times(b, cross), a_t) + times(
            times(a, cross) + times(b, last), b_t
        )

    next_gram = inner(a1, a1_t, b1, b1_t, bb, yb, yy)
    a2 = a1 + times(next_gram, inverse_bb)
    a2_t = a1_t + times(inverse_bb, next_gram)
    curvature = inner(a2, a2_t, b1, b1_t, yb + SHIFT * bb, yy + SHIFT * yb, wy + SHIFT * yy)
    (inverse_curvature,), eye = inverses([curvature])
    last_t = times(next_gram, inverse_curvature)
    base, mid = base_ref[...], mid_ref[...]
    top = received[:, :tile] + shifted_ref[...] * mid
    from_mid = times(last_t, b1)
    from_base = times(last_t, a2)
    solution_ref[...] = times(step_t + from_base, base) + times(from_mid, mid)
    residual_ref[...] = (
        times(a1 - SHIFT * from_base, base)
        + times(b1 - from_base - SHIFT * from_mid, mid)
        - times(from_mid, top)
    )


def local(kernel_codes, tile_scales, kernel_diagonal, noise_variance, targets):
    rhs, tile = targets.shape
    slots = kernel_codes.shape[0] // (tile // 2)
    width = tile // LANES
    size = rhs * width
    row_count = lax.axis_size("row")
    col_count = lax.axis_size("col")
    side = slots * slots
    planes = col_count // side
    row_index = lax.axis_index("row")
    col_index = lax.axis_index("col")
    plane, spot = col_index // side, col_index % side
    place = jnp.stack(
        [
            col_index - row_index * slots,
            row_index,
            plane,
            spot // slots,
            spot,
            row_index // (row_count // planes),
            plane * (row_count // planes) + spot // slots,
        ]
    ).astype(jnp.int32)
    near = [[first * side + index for index in range(side)] for first in range(planes)]
    deep = [
        [row * col_count + first * side + index for first in range(planes) for row in range(row_count)]
        for index in range(side)
    ]
    deep_count = planes * row_count
    shifted = (lax.reduce_precision(kernel_diagonal, 8, 7) + (noise_variance - SHIFT))[None, :]

    def exchange_near(values):
        return lax.all_to_all(values, "col", 0, 0, axis_index_groups=near)

    def exchange_deep(values):
        return lax.all_to_all(values, ("row", "col"), 0, 0, axis_index_groups=deep)

    def exchange_row(values):
        return lax.all_to_all(values, "row", 0, 0)

    slab = slab_spec(kernel_codes, slots)
    vector = whole((rhs, tile))
    scale_block = (tile_scales.shape[0] // slots, tile_scales.shape[1])
    slabs, outgoing, extra = pl.pallas_call(
        first_rows_kernel,
        grid=(slots,),
        in_specs=[SMEM, slab, pl.BlockSpec(scale_block, lambda slot: (slot, 0)), vector],
        out_specs=[
            slab,
            pl.BlockSpec((slots, 1, size + width, LANES), lambda slot: (0, slot, 0, 0)),
            vector,
        ],
        out_shape=[
            struct(kernel_codes.shape, BF16),
            struct((slots, slots, size + width, LANES), BF16),
            struct((rhs, tile), F32),
        ],
        compiler_params=PARAMS,
        name="first_rows",
    )(place, kernel_codes, tile_scales, targets)
    received = exchange_near(outgoing.reshape(side, size + width, LANES))
    relayed = plain(
        relay_kernel,
        struct((deep_count, slots + 1, width, LANES), BF16),
        "relay",
        received,
        scalars=False,
    )
    received = exchange_deep(relayed)
    message = pl.pallas_call(
        first_own_kernel,
        grid=(slots,),
        in_specs=[SMEM, slab, whole(received.shape), vector, vector],
        out_specs=whole((row_count, size + width, LANES)),
        out_shape=struct((row_count, size + width, LANES), BF16),
        scratch_shapes=[pltpu.VMEM((rhs, tile), F32), pltpu.VMEM((rhs, slots * tile), BF16)],
        compiler_params=PARAMS,
        name="first_own",
    )(place, slabs, received, targets, extra)
    received = exchange_row(message)
    mid, own, outgoing = plain(
        combine_kernel,
        [struct((rhs, tile), F32), struct((rhs, tile), BF16), struct((side, width, LANES), BF16)],
        "combine",
        place,
        received,
        targets,
        shifted,
    )
    received = exchange_near(outgoing)
    sent, extra = pl.pallas_call(
        second_rows_kernel,
        grid=(slots,),
        in_specs=[SMEM, slab, vector],
        out_specs=[pl.BlockSpec((1, rhs, tile), lambda slot: (slot, 0, 0)), vector],
        out_shape=[struct((slots, rhs, tile), BF16), struct((rhs, tile), F32)],
        compiler_params=PARAMS,
        name="second_rows",
    )(place, slabs, own)
    on_mid = jnp.dot(
        jnp.concatenate([mid, shifted * mid]), mid.T, precision=lax.Precision.HIGHEST
    )
    on_base = jnp.dot(
        jnp.concatenate([targets, mid]), targets.T, precision=lax.Precision.HIGHEST
    )
    grams = jnp.concatenate(
        [jnp.zeros((rhs, rhs), F32), on_base[:rhs], on_base[rhs:], on_mid[:rhs], on_mid[rhs:]], axis=1
    )
    grams = jnp.pad(grams * (1.0 / row_count), ((0, 0), (0, LANES - 5 * rhs)))
    relayed = jnp.broadcast_to(
        received.reshape(1, slots, slots, width, LANES),
        (deep_count // slots, slots, slots, width, LANES),
    ).reshape(deep_count, slots, width, LANES)
    received = exchange_deep(relayed)
    height = width + 4
    outgoing = pl.pallas_call(
        second_own_kernel,
        grid=(slots,),
        in_specs=[
            SMEM,
            slab,
            whole(received.shape),
            vector,
            vector,
            whole(sent.shape),
            whole(grams.shape),
        ],
        out_specs=whole((deep_count, slots + 1, height, LANES)),
        out_shape=struct((deep_count, slots + 1, height, LANES), BF16),
        scratch_shapes=[
            pltpu.VMEM((rhs, tile), F32),
            pltpu.VMEM((rhs, slots * tile), BF16),
            pltpu.VMEM((rhs, LANES), F32),
        ],
        compiler_params=PARAMS,
        name="second_own",
    )(place, slabs, received, own, extra, sent, grams)
    received = exchange_deep(outgoing)
    outgoing = plain(
        functools.partial(reduce_kernel, width),
        struct((side, height, LANES), BF16),
        "reduce_planes",
        place,
        received,
    )
    received = exchange_near(outgoing)
    outgoing = plain(
        functools.partial(finish_reduce_kernel, width),
        struct((row_count, height, LANES), F32),
        "reduce_tiles",
        received,
        scalars=False,
    )
    received = exchange_row(outgoing)
    return tuple(
        plain(
            final_kernel,
            [struct((rhs, tile), F32)] * 2,
            "small_solves",
            received,
            targets,
            mid,
            shifted,
            scalars=False,
        )
    )


def solution(mesh):
    in_specs = (P("row", "col"), P("row", "col"), P("col"), P("col"), P(None, "col"))
    out_specs = (P(None, "col"), P(None, "col"))
    return jax.shard_map(local, mesh=mesh, in_specs=in_specs, out_specs=out_specs, check_vma=False)
```

```python
import functools

import jax
import jax.numpy as jnp
from jax import lax
from jax.experimental import pallas as pl
from jax.experimental.pallas import tpu as pltpu
from jax.sharding import PartitionSpec as P

F32 = jnp.float32
BF16 = jnp.bfloat16
SHIFT = 3.0
VMEM_LIMIT = 56 * 1024 * 1024


def spread_scales(scales_ref, wide_ref):
    col_blocks = scales_ref.shape[0]
    cols = wide_ref.shape[1]
    lane_block = lax.broadcasted_iota(jnp.int32, (col_blocks, cols), 1) // (cols // col_blocks)
    own_block = lax.broadcasted_iota(jnp.int32, (col_blocks, cols), 0)
    spread = jnp.where(lane_block == own_block, 1.0, 0.0).astype(F32)
    wide_ref[...] = lax.dot_general(
        scales_ref[...],
        spread,
        (((0,), (0,)), ((), ())),
        precision=lax.Precision.HIGHEST,
        preferred_element_type=F32,
    )


def dequantize_slot(slot, codes_ref, wide_ref, out_ref):
    rows = codes_ref.shape[0]
    block_rows = wide_ref.shape[0] // pl.num_programs(0)
    order = rows // block_rows
    start = pl.multiple_of(slot * block_rows, 8)
    wide = wide_ref[pl.ds(start, block_rows), :]
    for block in range(block_rows):
        part = slice(block * order, (block + 1) * order)
        out_ref[part, :] = (codes_ref[part, :].astype(F32) * wide[block : block + 1, :]).astype(BF16)


NT = (((1,), (1,)), ((), ()))


def dot(left, right):
    return jnp.dot(left, right, preferred_element_type=F32)


def dot_t(left, right):
    return lax.dot_general(left, right, NT, preferred_element_type=F32)


def triangles(slab_ref):
    half = slab_ref.shape[0]
    mixed = slab_ref[:, :half]
    row = lax.broadcasted_iota(jnp.int32, (half, half), 0)
    col = lax.broadcasted_iota(jnp.int32, (half, half), 1)
    zero = jnp.zeros_like(mixed)
    return jnp.where(row > col, mixed, zero), jnp.where(row < col, mixed, zero)


LANES = 128


def to_tiles(values):
    count = values.shape[1] // LANES
    return jnp.concatenate(
        [values[:, part * LANES : (part + 1) * LANES] for part in range(count)], axis=0
    )


def from_tiles(tiles, rhs):
    count = tiles.shape[0] // rhs
    return jnp.concatenate(
        [tiles[part * rhs : (part + 1) * rhs, :] for part in range(count)], axis=1
    )


def row_tiles(values):
    return values.reshape(values.shape[0], values.shape[1] // LANES, LANES)


def flat_rows(tiles):
    return tiles.reshape(tiles.shape[0], tiles.shape[1] * LANES)


def share_of(values, row_index):
    tiles = row_tiles(values)
    row = lax.broadcasted_iota(jnp.int32, tiles.shape, 0)
    return jnp.sum(jnp.where(row == row_index, tiles, 0.0), axis=0)


def toward_rows(slot, offset, slab_ref, own, put, extra_ref):
    half, tile = slab_ref.shape
    rhs = own.shape[0]

    @pl.when(slot == 0)
    def _():
        extra_ref[...] = jnp.zeros_like(extra_ref)

    @pl.when(slot < offset)
    def _():
        second = dot_t(own, slab_ref[...])
        put(jnp.concatenate([second, jnp.zeros((rhs, tile - half), F32)], axis=1))

    @pl.when(slot > offset)
    def _():
        put(dot(own[:, half:], slab_ref[...]))

    @pl.when(slot == offset)
    def _():
        low, high = triangles(slab_ref)
        head, tail = own[:, :half], own[:, half:]
        extra_ref[:, :half] = dot_t(head, low) + dot_t(tail, slab_ref[:, half:])
        extra_ref[:, half:] = dot_t(tail, high)
        put(jnp.zeros((rhs, tile), F32))


def first_rows_kernel(
    place_ref, codes_ref, scales_ref, base_ref, slab_ref, out_ref, extra_ref, wide_ref
):
    @pl.when(pl.program_id(0) == 0)
    def _():
        spread_scales(scales_ref, wide_ref)

    dequantize_slot(pl.program_id(0), codes_ref, wide_ref, slab_ref)
    rhs, tile = base_ref.shape
    size = rhs * tile // LANES
    base = base_ref[...]
    share = share_of(base, place_ref[1]).astype(BF16)
    for copy in range(out_ref.shape[0]):
        out_ref[copy, 0, size:, :] = share

    def put(values):
        tiles = to_tiles(values).astype(BF16)
        for copy in range(out_ref.shape[0]):
            out_ref[copy, 0, :size, :] = tiles

    toward_rows(pl.program_id(0), place_ref[0], slab_ref, base.astype(BF16), put, extra_ref)


def second_rows_kernel(
    copies, place_ref, slab_ref, own_ref, base_ref, mid_ref, shifted_ref, out_ref, extra_ref, sums_ref
):
    rhs = own_ref.shape[0]

    @pl.when(pl.program_id(0) == 0)
    def _():
        base, mid = base_ref[...], mid_ref[...]
        exact = functools.partial(
            lax.dot_general,
            dimension_numbers=NT,
            precision=lax.Precision.HIGHEST,
            preferred_element_type=F32,
        )
        on_base = exact(jnp.concatenate([base, mid]), base)
        on_mid = exact(jnp.concatenate([mid, shifted_ref[...] * mid]), mid)
        sums_ref[...] = jnp.zeros_like(sums_ref)
        for part, value in enumerate((on_base[:rhs], on_base[rhs:], on_mid[:rhs], on_mid[rhs:])):
            sums_ref[:, (part + 1) * rhs : (part + 2) * rhs] = value * (1.0 / copies)

    def put(values):
        out_ref[0, :, :] = values.astype(BF16)

    toward_rows(pl.program_id(0), place_ref[0], slab_ref, own_ref[...], put, extra_ref)


def relay_kernel(received_ref, out_ref):
    senders, height, lanes = received_ref.shape
    copies, parts, width, lanes = out_ref.shape
    size = height - width
    slots = parts - 1
    rhs = size // width
    reduced = received_ref[0, :size, :].astype(F32)
    for sender in range(1, senders):
        reduced = reduced + received_ref[sender, :size, :].astype(F32)
    rows = row_tiles(from_tiles(reduced, rhs)).astype(BF16)
    for copy in range(copies):
        first = (copy % (senders // slots)) * slots
        out_ref[copy, :slots, :, :] = received_ref[first : first + slots, size:, :]
        out_ref[copy, slots, :, :] = rows[copy % rhs]


def gather_rows(place_ref, received_ref, rows_ref, tile, slots):
    rhs = rows_ref.shape[0]
    start = place_ref[5] * rhs
    for part in range(slots):
        piece = received_ref[pl.ds(start, rhs), part, :, :].astype(F32)
        rows_ref[:, part * tile : (part + 1) * tile] = flat_rows(piece).astype(BF16)


def toward_own(slot, offset, slab_ref, rows_ref, own, total_ref):
    half, tile = slab_ref.shape
    lanes = pl.multiple_of(slot * tile, tile)

    @pl.when(slot < offset)
    def _():
        total_ref[...] += dot(rows_ref[:, pl.ds(lanes, half)], slab_ref[...])

    @pl.when(slot > offset)
    def _():
        total_ref[:, half:] += dot_t(rows_ref[:, pl.ds(lanes, tile)], slab_ref[...])

    @pl.when(slot == offset)
    def _():
        low, high = triangles(slab_ref)
        head, tail = own[:, :half], own[:, half:]
        total_ref[:, :half] += dot(head, low)
        total_ref[:, half:] += dot(head, slab_ref[:, half:]) + dot(tail, high)


def first_own_kernel(
    place_ref, slab_ref, received_ref, base_ref, extra_ref, out_ref, total_ref, rows_ref
):
    slot, slots = pl.program_id(0), rows_ref.shape[1] // base_ref.shape[1]
    rhs, tile = base_ref.shape

    @pl.when(slot == 0)
    def _():
        total_ref[...] = extra_ref[...]
        gather_rows(place_ref, received_ref, rows_ref, tile, slots)

    toward_own(slot, place_ref[0], slab_ref, rows_ref, base_ref[...].astype(BF16), total_ref)

    @pl.when(slot == slots - 1)
    def _():
        size = rhs * tile // LANES
        source = place_ref[6]
        planes = received_ref.shape[0] // rhs
        reduced = received_ref[source, slots, :, :].astype(F32)
        for plane in range(1, planes):
            reduced = reduced + received_ref[plane * rhs + source, slots, :, :].astype(F32)
        reduced = reduced.astype(BF16)
        tiles = to_tiles(total_ref[...]).astype(BF16)
        for copy in range(out_ref.shape[0]):
            out_ref[copy, :size, :] = tiles
            out_ref[copy, size:, :] = reduced


def combine_kernel(place_ref, received_ref, base_ref, shifted_ref, mid_ref, own_ref, out_ref):
    rhs, tile = base_ref.shape
    size = rhs * tile // LANES
    total = received_ref[0, :size, :].astype(F32)
    for sender in range(1, received_ref.shape[0]):
        total = total + received_ref[sender, :size, :].astype(F32)
    others = flat_rows(received_ref[:, size:, :].astype(F32))
    mid = (from_tiles(total, rhs) + others) + shifted_ref[...] * base_ref[...]
    mid_ref[...] = mid
    own_ref[...] = mid.astype(BF16)
    share = share_of(mid, place_ref[1]).astype(BF16)
    for copy in range(out_ref.shape[0]):
        out_ref[copy, :, :] = share


def three_parts(values):
    first = values.astype(BF16).astype(F32)
    rest = values - first
    second = rest.astype(BF16).astype(F32)
    return first, second, rest - second


def pack_sums(values, used):
    parts = [part[:, :used] for part in three_parts(values)]
    blank = jnp.zeros((values.shape[0], LANES - 3 * used), F32)
    return jnp.concatenate(parts + [blank], axis=1).astype(BF16)


def unpack_sums(values, used):
    return (values[:, :used] + values[:, used : 2 * used]) + values[:, 2 * used : 3 * used]


def pair_kernel(
    place_ref, received_ref, own_ref, extra_ref, sent_ref, grams_ref, out_ref, rows_ref, sums_ref
):
    rhs, tile = own_ref.shape
    slots = sent_ref.shape[0]
    size = rhs * tile // LANES
    gather_rows(place_ref, received_ref, rows_ref, tile, slots)
    pair = dot_t(extra_ref[...].astype(BF16), own_ref[...])
    for part in range(slots):
        pair = pair + dot_t(sent_ref[part], rows_ref[:, part * tile : (part + 1) * tile])
    sums_ref[...] = grams_ref[...]
    sums_ref[:, :rhs] = pair
    packed = pack_sums(sums_ref[...], 5 * rhs)
    for target in range(out_ref.shape[0]):
        out_ref[target, size:, :] = packed
    for part in range(slots):
        tiles = to_tiles(sent_ref[part].astype(F32)).astype(BF16)
        for target in range(part, out_ref.shape[0], slots):
            out_ref[target, :size, :] = tiles


def second_own_kernel(place_ref, slab_ref, rows_ref, own_ref, extra_ref, out_ref, total_ref):
    slot = pl.program_id(0)

    @pl.when(slot == 0)
    def _():
        total_ref[...] = extra_ref[...]

    toward_own(slot, place_ref[0], slab_ref, rows_ref, own_ref[...], total_ref)

    @pl.when(slot == pl.num_programs(0) - 1)
    def _():
        out_ref[...] = to_tiles(total_ref[...])


def summed(received_ref):
    total = received_ref[0, :, :].astype(F32)
    for sender in range(1, received_ref.shape[0]):
        total = total + received_ref[sender, :, :].astype(F32)
    return total


def join_kernel(place_ref, received_ref, own_ref, out_ref):
    size, lanes = own_ref.shape
    rhs = out_ref.shape[1] - size
    total = summed(received_ref)
    packed = pack_sums(unpack_sums(total[size:, :], 5 * rhs), 5 * rhs)
    planes = out_ref.shape[0] // rhs
    for plane in range(planes):
        for_own = place_ref[2] == plane
        for_row = jnp.logical_and(place_ref[5] == plane, place_ref[3] == place_ref[7])
        value = jnp.where(for_own, own_ref[...], 0.0) + jnp.where(for_row, total[:size, :], 0.0)
        value = value.astype(BF16)
        for copy in range(rhs):
            out_ref[plane * rhs + copy, :size, :] = value
            out_ref[plane * rhs + copy, size:, :] = packed


def whole(shape):
    return pl.BlockSpec(shape, lambda slot: (0,) * len(shape))


SMEM = pl.BlockSpec(memory_space=pltpu.SMEM)
PARAMS = pltpu.CompilerParams(vmem_limit_bytes=VMEM_LIMIT)


def struct(shape, dtype):
    return jax.ShapeDtypeStruct(shape, dtype)


def plain(kernel, outs, name, *operands, scalars=True):
    specs = [pl.BlockSpec(memory_space=pltpu.VMEM)] * len(operands)
    if scalars:
        specs[0] = SMEM
    return pl.pallas_call(
        kernel, in_specs=specs, out_shape=outs, compiler_params=PARAMS, name=name
    )(*operands)


def slab_spec(codes, slots):
    return pl.BlockSpec((codes.shape[0] // slots, codes.shape[1]), lambda slot: (slot, 0))


def times(left, right):
    total = left[:, 0:1] * right[0:1, :]
    for index in range(1, left.shape[1]):
        total = total + left[:, index : index + 1] * right[index : index + 1, :]
    return total


def inverses(matrices):
    size = matrices[0].shape[0]
    row = lax.broadcasted_iota(jnp.int32, (size, size), 0)
    col = lax.broadcasted_iota(jnp.int32, (size, size), 1)
    eye = jnp.where(row == col, 1.0, 0.0).astype(F32)
    work = [(matrix, eye) for matrix in matrices]
    for step in range(size):
        here = row == step
        following = []
        for left, right in work:
            scale = 1.0 / left[step : step + 1, step : step + 1]
            left_row = left[step : step + 1, :] * scale
            right_row = right[step : step + 1, :] * scale
            column = left[:, step : step + 1]
            following.append(
                (
                    jnp.where(here, left_row, left - column * left_row),
                    jnp.where(here, right_row, right - column * right_row),
                )
            )
        work = following
    return [right for left, right in work], eye


def final_kernel(
    received_ref, base_ref, mid_ref, shifted_ref, solution_ref, residual_ref
):
    rhs, tile = base_ref.shape
    size = rhs * tile // LANES
    total = summed(received_ref)
    gram = unpack_sums(total[size:, :], 5 * rhs)
    half_wy, bb, yb, yy, wy = (gram[:, index * rhs : (index + 1) * rhs] for index in range(5))
    wy = wy + (half_wy + half_wy.T)
    curvature = yb + SHIFT * bb
    (inverse_curvature, inverse_bb), eye = inverses([curvature, bb])
    step_t = times(bb, inverse_curvature)
    step = times(inverse_curvature, bb)
    a1, a1_t = eye - SHIFT * step_t, eye - SHIFT * step
    b1, b1_t = -step_t, -step

    def inner(a, a_t, b, b_t, first, cross, last):
        return times(times(a, first) + times(b, cross), a_t) + times(
            times(a, cross) + times(b, last), b_t
        )

    next_gram = inner(a1, a1_t, b1, b1_t, bb, yb, yy)
    a2 = a1 + times(next_gram, inverse_bb)
    a2_t = a1_t + times(inverse_bb, next_gram)
    curvature = inner(a2, a2_t, b1, b1_t, yb + SHIFT * bb, yy + SHIFT * yb, wy + SHIFT * yy)
    (inverse_curvature,), eye = inverses([curvature])
    last_t = times(next_gram, inverse_curvature)
    base, mid = base_ref[...], mid_ref[...]
    top = from_tiles(total[:size, :], rhs) + shifted_ref[...] * mid
    from_mid = times(last_t, b1)
    from_base = times(last_t, a2)
    solution_ref[...] = times(step_t + from_base, base) + times(from_mid, mid)
    residual_ref[...] = (
        times(a1 - SHIFT * from_base, base)
        + times(b1 - from_base - SHIFT * from_mid, mid)
        - times(from_mid, top)
    )


def local(kernel_codes, tile_scales, kernel_diagonal, noise_variance, targets):
    rhs, tile = targets.shape
    slots = kernel_codes.shape[0] // (tile // 2)
    width = tile // LANES
    size = rhs * width
    row_count = lax.axis_size("row")
    col_count = lax.axis_size("col")
    side = slots * slots
    planes = col_count // side
    row_index = lax.axis_index("row")
    col_index = lax.axis_index("col")
    plane, spot = col_index // side, col_index % side
    place = jnp.stack(
        [
            col_index - row_index * slots,
            row_index,
            plane,
            spot // slots,
            spot,
            row_index // (row_count // planes),
            plane * (row_count // planes) + spot // slots,
            row_index % (row_count // planes),
        ]
    ).astype(jnp.int32)
    near = [[first * side + index for index in range(side)] for first in range(planes)]
    deep = [
        [row * col_count + first * side + index for first in range(planes) for row in range(row_count)]
        for index in range(side)
    ]
    deep_count = planes * row_count
    shifted = (lax.reduce_precision(kernel_diagonal, 8, 7) + (noise_variance - SHIFT))[None, :]

    def exchange_near(values):
        return lax.all_to_all(values, "col", 0, 0, axis_index_groups=near)

    def exchange_deep(values):
        return lax.all_to_all(values, ("row", "col"), 0, 0, axis_index_groups=deep)

    def exchange_row(values):
        return lax.all_to_all(values, "row", 0, 0)

    slab = slab_spec(kernel_codes, slots)
    vector = whole((rhs, tile))
    scales = tile_scales.T
    slabs, outgoing, extra = pl.pallas_call(
        first_rows_kernel,
        grid=(slots,),
        in_specs=[SMEM, slab, whole(scales.shape), vector],
        out_specs=[
            slab,
            pl.BlockSpec((slots, 1, size + width, LANES), lambda slot: (0, slot, 0, 0)),
            vector,
        ],
        out_shape=[
            struct(kernel_codes.shape, BF16),
            struct((slots, slots, size + width, LANES), BF16),
            struct((rhs, tile), F32),
        ],
        scratch_shapes=[pltpu.VMEM((tile_scales.shape[0], tile), F32)],
        compiler_params=PARAMS,
        name="first_rows",
    )(place, kernel_codes, scales, targets)
    received = exchange_near(outgoing.reshape(side, size + width, LANES))
    relayed = plain(
        relay_kernel,
        struct((deep_count, slots + 1, width, LANES), BF16),
        "relay",
        received,
        scalars=False,
    )
    received = exchange_deep(relayed)
    message = pl.pallas_call(
        first_own_kernel,
        grid=(slots,),
        in_specs=[SMEM, slab, whole(received.shape), vector, vector],
        out_specs=whole((row_count, size + width, LANES)),
        out_shape=struct((row_count, size + width, LANES), BF16),
        scratch_shapes=[pltpu.VMEM((rhs, tile), F32), pltpu.VMEM((rhs, slots * tile), BF16)],
        compiler_params=PARAMS,
        name="first_own",
    )(place, slabs, received, targets, extra)
    received = exchange_row(message)
    mid, own, outgoing = plain(
        combine_kernel,
        [struct((rhs, tile), F32), struct((rhs, tile), BF16), struct((side, width, LANES), BF16)],
        "combine",
        place,
        received,
        targets,
        shifted,
    )
    received = exchange_near(outgoing)
    sent, extra, grams = pl.pallas_call(
        functools.partial(second_rows_kernel, row_count),
        grid=(slots,),
        in_specs=[SMEM, slab, vector, vector, vector, whole(shifted.shape)],
        out_specs=[
            pl.BlockSpec((1, rhs, tile), lambda slot: (slot, 0, 0)),
            vector,
            whole((rhs, LANES)),
        ],
        out_shape=[
            struct((slots, rhs, tile), BF16),
            struct((rhs, tile), F32),
            struct((rhs, LANES), F32),
        ],
        compiler_params=PARAMS,
        name="second_rows",
    )(place, slabs, own, targets, mid, shifted)
    relayed = jnp.broadcast_to(
        received.reshape(1, slots, slots, width, LANES),
        (deep_count // slots, slots, slots, width, LANES),
    ).reshape(deep_count, slots, width, LANES)
    received = exchange_deep(relayed)
    outgoing, rows = pl.pallas_call(
        pair_kernel,
        in_specs=[SMEM] + [pl.BlockSpec(memory_space=pltpu.VMEM)] * 5,
        out_shape=[
            struct((side, size + rhs, LANES), BF16),
            struct((rhs, slots * tile), BF16),
        ],
        scratch_shapes=[pltpu.VMEM((rhs, LANES), F32)],
        compiler_params=PARAMS,
        name="pair",
    )(place, received, own, extra, sent, grams)
    received = exchange_near(outgoing)
    total = pl.pallas_call(
        second_own_kernel,
        grid=(slots,),
        in_specs=[SMEM, slab, whole(rows.shape), vector, vector],
        out_specs=whole((size, LANES)),
        out_shape=struct((size, LANES), F32),
        scratch_shapes=[pltpu.VMEM((rhs, tile), F32)],
        compiler_params=PARAMS,
        name="second_own",
    )(place, slabs, rows, own, extra)
    outgoing = plain(
        join_kernel,
        struct((deep_count, size + rhs, LANES), BF16),
        "join",
        place,
        received,
        total,
    )
    received = exchange_deep(outgoing)
    return tuple(
        plain(
            final_kernel,
            [struct((rhs, tile), F32)] * 2,
            "small_solves",
            received,
            targets,
            mid,
            shifted,
            scalars=False,
        )
    )


def solution(mesh):
    in_specs = (P("row", "col"), P("row", "col"), P("col"), P("col"), P(None, "col"))
    out_specs = (P(None, "col"), P(None, "col"))
    return jax.shard_map(local, mesh=mesh, in_specs=in_specs, out_specs=out_specs, check_vma=False)
```

```python
import functools

import jax
import jax.numpy as jnp
from jax import lax
from jax.experimental import pallas as pl
from jax.experimental.pallas import tpu as pltpu
from jax.sharding import PartitionSpec as P

F32 = jnp.float32
BF16 = jnp.bfloat16
SHIFT = 3.0
VMEM_LIMIT = 32 * 1024 * 1024


def spread_scales(scales_ref, wide_ref):
    col_blocks = scales_ref.shape[0]
    cols = wide_ref.shape[1]
    lane_block = lax.broadcasted_iota(jnp.int32, (col_blocks, cols), 1) // (cols // col_blocks)
    own_block = lax.broadcasted_iota(jnp.int32, (col_blocks, cols), 0)
    spread = jnp.where(lane_block == own_block, 1.0, 0.0).astype(F32)
    wide_ref[...] = lax.dot_general(
        scales_ref[...],
        spread,
        (((0,), (0,)), ((), ())),
        precision=lax.Precision.HIGHEST,
        preferred_element_type=F32,
    )


def dequantize_slot(slot, slots, codes_ref, wide_ref, slab_ref):
    rows = codes_ref.shape[0] // slots
    block_rows = wide_ref.shape[0] // slots
    order = rows // block_rows
    for block in range(slot * block_rows, (slot + 1) * block_rows):
        part = slice(block * order, (block + 1) * order)
        wide = wide_ref[block : block + 1, :]
        slab_ref[part, :] = (codes_ref[part, :].astype(F32) * wide).astype(BF16)


NT = (((1,), (1,)), ((), ()))


def dot(left, right):
    return jnp.dot(left, right, preferred_element_type=F32)


def dot_t(left, right):
    return lax.dot_general(left, right, NT, preferred_element_type=F32)


def triangles(slab_ref):
    half = slab_ref.shape[0]
    mixed = slab_ref[:, :half]
    row = lax.broadcasted_iota(jnp.int32, (half, half), 0)
    col = lax.broadcasted_iota(jnp.int32, (half, half), 1)
    zero = jnp.zeros_like(mixed)
    return jnp.where(row > col, mixed, zero), jnp.where(row < col, mixed, zero)


LANES = 128


def to_tiles(values):
    count = values.shape[1] // LANES
    return jnp.concatenate(
        [values[:, part * LANES : (part + 1) * LANES] for part in range(count)], axis=0
    )


def from_tiles(tiles, rhs):
    count = tiles.shape[0] // rhs
    return jnp.concatenate(
        [tiles[part * rhs : (part + 1) * rhs, :] for part in range(count)], axis=1
    )


def row_tiles(values):
    return values.reshape(values.shape[0], values.shape[1] // LANES, LANES)


def flat_rows(tiles):
    return tiles.reshape(tiles.shape[0], tiles.shape[1] * LANES)


def share_of(values, row_index):
    tiles = row_tiles(values)
    row = lax.broadcasted_iota(jnp.int32, tiles.shape, 0)
    return jnp.sum(jnp.where(row == row_index, tiles, 0.0), axis=0)


def toward_rows(slot, offset, slab_ref, own, put, extra_ref, beside):
    half, tile = slab_ref.shape
    rhs = own.shape[0]

    @pl.when(slot < offset)
    def _():
        second = dot_t(own, slab_ref[...])
        beside()
        put(jnp.concatenate([second, jnp.zeros((rhs, tile - half), F32)], axis=1))

    @pl.when(slot > offset)
    def _():
        first = dot(own[:, half:], slab_ref[...])
        beside()
        put(first)

    @pl.when(slot == offset)
    def _():
        low, high = triangles(slab_ref)
        head, tail = own[:, :half], own[:, half:]
        extra_ref[:, :half] = dot_t(head, low) + dot_t(tail, slab_ref[:, half:])
        extra_ref[:, half:] = dot_t(tail, high)
        beside()
        put(jnp.zeros((rhs, tile), F32))


def slot_copies(source_ref, target_ref, semaphores):
    slots = semaphores.shape[0]
    half = source_ref.shape[0] // slots
    copies = []
    for slot in range(slots):
        part = pl.ds(slot * half, half)
        copies.append(
            pltpu.make_async_copy(
                source_ref.at[part, :], target_ref.at[part, :], semaphores.at[slot]
            )
        )
    return copies


def slot_of(slab_ref, slot, half):
    return slab_ref.at[pl.ds(slot * half, half), :]


def first_rows_kernel(
    place_ref,
    codes_hbm,
    scales_ref,
    base_ref,
    shifted_ref,
    slab_ref,
    stored_hbm,
    out_ref,
    extra_ref,
    scaled_ref,
    wide_ref,
    codes_ref,
    arrived,
    stored,
):
    slots = out_ref.shape[1]
    half = slab_ref.shape[0] // slots
    copies = slot_copies(codes_hbm, codes_ref, arrived)
    stores = slot_copies(slab_ref, stored_hbm, stored)
    for copy in copies:
        copy.start()
    spread_scales(scales_ref, wide_ref)
    rhs, tile = base_ref.shape
    size = rhs * tile // LANES
    base = base_ref[...]
    scaled_ref[...] = shifted_ref[...] * base
    own = base.astype(BF16)
    share = share_of(base, place_ref[1]).astype(BF16)
    for copy in range(slots):
        for slot in range(slots):
            out_ref[copy, slot, size:, :] = share
    extra_ref[...] = jnp.zeros_like(extra_ref)
    copies[0].wait()
    dequantize_slot(0, slots, codes_ref, wide_ref, slab_ref)
    stores[0].start()
    for slot in range(slots):
        if slot + 1 < slots:
            copies[slot + 1].wait()

        def beside(slot=slot):
            if slot + 1 < slots:
                dequantize_slot(slot + 1, slots, codes_ref, wide_ref, slab_ref)

        def put(values, slot=slot):
            tiles = to_tiles(values).astype(BF16)
            for copy in range(slots):
                out_ref[copy, slot, :size, :] = tiles

        view = slot_of(slab_ref, slot, half)
        toward_rows(slot, place_ref[0], view, own, put, extra_ref, beside)
        if slot + 1 < slots:
            stores[slot + 1].start()
    for store in stores:
        store.wait()


def second_rows_kernel(
    copies, place_ref, slab_hbm, own_ref, base_ref, mid_ref, shifted_ref,
    out_ref, extra_ref, sums_ref, slab_ref, arrived
):
    fetches = slot_copies(slab_hbm, slab_ref, arrived)
    for fetch in fetches:
        fetch.start()
    rhs = own_ref.shape[0]
    base, mid = base_ref[...], mid_ref[...]
    exact = functools.partial(
        lax.dot_general,
        dimension_numbers=NT,
        precision=lax.Precision.HIGHEST,
        preferred_element_type=F32,
    )
    on_base = exact(jnp.concatenate([base, mid]), base)
    on_mid = exact(jnp.concatenate([mid, shifted_ref[...] * mid]), mid)
    sums_ref[...] = jnp.zeros_like(sums_ref)
    for part, value in enumerate((on_base[:rhs], on_base[rhs:], on_mid[:rhs], on_mid[rhs:])):
        sums_ref[:, (part + 1) * rhs : (part + 2) * rhs] = value * (1.0 / copies)
    extra_ref[...] = jnp.zeros_like(extra_ref)
    for slot in range(out_ref.shape[0]):

        def put(values, slot=slot):
            out_ref[slot, :, :] = values.astype(BF16)

        half = slab_ref.shape[0] // out_ref.shape[0]
        view = slot_of(slab_ref, slot, half)
        fetches[slot].wait()
        toward_rows(slot, place_ref[0], view, own_ref[...], put, extra_ref, lambda: None)


def relay_kernel(width, received_ref, out_ref):
    senders, height, lanes = received_ref.shape
    copies, full, lanes = out_ref.shape
    size = height - width
    slots = full // width - 1
    rhs = size // width
    reduced = received_ref[0, :size, :].astype(F32)
    for sender in range(1, senders):
        reduced = reduced + received_ref[sender, :size, :].astype(F32)
    rows = row_tiles(from_tiles(reduced, rhs)).astype(BF16)
    groups = []
    for first in range(0, senders, slots):
        pieces = [received_ref[first + part, size:, :].astype(F32) for part in range(slots)]
        groups.append(jnp.concatenate(pieces, axis=0).astype(BF16))
    for copy in range(copies):
        out_ref[copy, : slots * width, :] = groups[copy % len(groups)]
        out_ref[copy, slots * width :, :] = rows[copy % rhs]


def spread_kernel(received_ref, out_ref):
    senders, width, lanes = received_ref.shape
    slots = out_ref.shape[1] // width
    for first in range(0, senders, slots):
        pieces = [received_ref[first + part].astype(F32) for part in range(slots)]
        group = jnp.concatenate(pieces, axis=0).astype(BF16)
        for copy in range(first // slots, out_ref.shape[0], senders // slots):
            out_ref[copy, :, :] = group


def gather_rows(place_ref, received_ref, rows_ref, tile, slots):
    rhs = rows_ref.shape[0]
    start = place_ref[5] * rhs
    size = slots * tile // LANES
    piece = received_ref[pl.ds(start, rhs), :size, :].astype(F32)
    rows_ref[...] = flat_rows(piece).astype(BF16)


def toward_own(slot, offset, slab_ref, rows_ref, own, total_ref):
    half, tile = slab_ref.shape
    lanes = pl.multiple_of(slot * tile, tile)

    @pl.when(slot < offset)
    def _():
        total_ref[...] += dot(rows_ref[:, pl.ds(lanes, half)], slab_ref[...])

    @pl.when(slot > offset)
    def _():
        total_ref[:, half:] += dot_t(rows_ref[:, pl.ds(lanes, tile)], slab_ref[...])

    @pl.when(slot == offset)
    def _():
        low, high = triangles(slab_ref)
        head, tail = own[:, :half], own[:, half:]
        total_ref[:, :half] += dot(head, low)
        total_ref[:, half:] += dot(head, slab_ref[:, half:]) + dot(tail, high)


def all_toward_own(place_ref, slab_ref, rows_ref, own, total_ref, fetches=None):
    slots = rows_ref.shape[1] // own.shape[1]
    half = slab_ref.shape[0] // slots
    for slot in range(slots):
        if fetches is not None:
            fetches[slot].wait()
        toward_own(slot, place_ref[0], slot_of(slab_ref, slot, half), rows_ref, own, total_ref)


def first_own_kernel(
    place_ref, slab_ref, received_ref, base_ref, extra_ref, out_ref, total_ref, rows_ref
):
    rhs, tile = base_ref.shape
    slots = rows_ref.shape[1] // tile
    width = tile // LANES
    total_ref[...] = extra_ref[...]
    gather_rows(place_ref, received_ref, rows_ref, tile, slots)
    all_toward_own(place_ref, slab_ref, rows_ref, base_ref[...].astype(BF16), total_ref)
    size = rhs * tile // LANES
    source = place_ref[6]
    planes = received_ref.shape[0] // rhs
    part = slice(slots * width, (slots + 1) * width)
    reduced = received_ref[source, part, :].astype(F32)
    for plane in range(1, planes):
        reduced = reduced + received_ref[plane * rhs + source, part, :].astype(F32)
    reduced = reduced.astype(BF16)
    tiles = to_tiles(total_ref[...]).astype(BF16)
    for copy in range(out_ref.shape[0]):
        out_ref[copy, :size, :] = tiles
        out_ref[copy, size:, :] = reduced


def combine_kernel(place_ref, received_ref, scaled_ref, mid_ref, own_ref, out_ref):
    rhs, tile = scaled_ref.shape
    size = rhs * tile // LANES
    total = received_ref[0, :size, :].astype(F32)
    for sender in range(1, received_ref.shape[0]):
        total = total + received_ref[sender, :size, :].astype(F32)
    others = flat_rows(received_ref[:, size:, :].astype(F32))
    mid = (from_tiles(total, rhs) + others) + scaled_ref[...]
    mid_ref[...] = mid
    own_ref[...] = mid.astype(BF16)
    share = share_of(mid, place_ref[1]).astype(BF16)
    for copy in range(out_ref.shape[0]):
        out_ref[copy, :, :] = share


def three_parts(values):
    first = values.astype(BF16).astype(F32)
    rest = values - first
    second = rest.astype(BF16).astype(F32)
    return first, second, rest - second


def pack_sums(values, used):
    parts = [part[:, :used] for part in three_parts(values)]
    blank = jnp.zeros((values.shape[0], LANES - 3 * used), F32)
    return jnp.concatenate(parts + [blank], axis=1).astype(BF16)


def unpack_sums(values, used):
    return (values[:, :used] + values[:, used : 2 * used]) + values[:, 2 * used : 3 * used]


def pair_kernel(
    place_ref, received_ref, own_ref, extra_ref, sent_ref, grams_ref, out_ref, rows_ref, sums_ref
):
    rhs, tile = own_ref.shape
    slots = sent_ref.shape[0]
    size = rhs * tile // LANES
    gather_rows(place_ref, received_ref, rows_ref, tile, slots)
    pair = dot_t(extra_ref[...].astype(BF16), own_ref[...])
    for part in range(slots):
        pair = pair + dot_t(sent_ref[part], rows_ref[:, part * tile : (part + 1) * tile])
    sums_ref[...] = grams_ref[...]
    sums_ref[:, :rhs] = pair
    packed = pack_sums(sums_ref[...], 5 * rhs)
    for target in range(out_ref.shape[0]):
        out_ref[target, size:, :] = packed
    for part in range(slots):
        tiles = to_tiles(sent_ref[part].astype(F32)).astype(BF16)
        for target in range(part, out_ref.shape[0], slots):
            out_ref[target, :size, :] = tiles


def second_own_kernel(
    place_ref, slab_hbm, rows_ref, own_ref, extra_ref, out_ref, total_ref, slab_ref, arrived
):
    fetches = slot_copies(slab_hbm, slab_ref, arrived)
    for fetch in fetches:
        fetch.start()
    total_ref[...] = extra_ref[...]
    all_toward_own(place_ref, slab_ref, rows_ref, own_ref[...], total_ref, fetches)
    out_ref[...] = to_tiles(total_ref[...])


def summed(received_ref):
    total = received_ref[0, :, :].astype(F32)
    for sender in range(1, received_ref.shape[0]):
        total = total + received_ref[sender, :, :].astype(F32)
    return total


def join_kernel(place_ref, received_ref, own_ref, out_ref):
    size, lanes = own_ref.shape
    rhs = out_ref.shape[1] - size
    total = summed(received_ref)
    packed = pack_sums(unpack_sums(total[size:, :], 5 * rhs), 5 * rhs)
    planes = out_ref.shape[0] // rhs
    for plane in range(planes):
        for_own = place_ref[2] == plane
        for_row = jnp.logical_and(place_ref[5] == plane, place_ref[3] == place_ref[7])
        value = jnp.where(for_own, own_ref[...], 0.0) + jnp.where(for_row, total[:size, :], 0.0)
        value = value.astype(BF16)
        for copy in range(rhs):
            out_ref[plane * rhs + copy, :size, :] = value
            out_ref[plane * rhs + copy, size:, :] = packed


SMEM = pl.BlockSpec(memory_space=pltpu.SMEM)
PARAMS = pltpu.CompilerParams(vmem_limit_bytes=VMEM_LIMIT)


def struct(shape, dtype):
    return jax.ShapeDtypeStruct(shape, dtype)


def in_place(values):
    return pltpu.with_memory_space_constraint(values, pltpu.VMEM)


def in_hbm(values):
    return pltpu.with_memory_space_constraint(values, pltpu.HBM)


def plain(kernel, outs, name, *operands, scalars=True, scratch=(), in_memory=()):
    specs = [pl.BlockSpec(memory_space=pltpu.VMEM)] * len(operands)
    if scalars:
        specs[0] = SMEM
    for index in in_memory:
        specs[index] = pl.BlockSpec(memory_space=pltpu.HBM)
    return pl.pallas_call(
        kernel,
        in_specs=specs,
        out_shape=outs,
        scratch_shapes=scratch,
        compiler_params=PARAMS,
        name=name,
    )(*operands)


def times(left, right):
    total = left[:, 0:1] * right[0:1, :]
    for index in range(1, left.shape[1]):
        total = total + left[:, index : index + 1] * right[index : index + 1, :]
    return total


def inverses(matrices):
    size = matrices[0].shape[0]
    row = lax.broadcasted_iota(jnp.int32, (size, size), 0)
    col = lax.broadcasted_iota(jnp.int32, (size, size), 1)
    eye = jnp.where(row == col, 1.0, 0.0).astype(F32)
    work = [(matrix, eye) for matrix in matrices]
    for step in range(size):
        here = row == step
        following = []
        for left, right in work:
            scale = 1.0 / left[step : step + 1, step : step + 1]
            left_row = left[step : step + 1, :] * scale
            right_row = right[step : step + 1, :] * scale
            column = left[:, step : step + 1]
            following.append(
                (
                    jnp.where(here, left_row, left - column * left_row),
                    jnp.where(here, right_row, right - column * right_row),
                )
            )
        work = following
    return [right for left, right in work], eye


def final_kernel(
    received_ref, base_ref, mid_ref, shifted_ref, solution_ref, residual_ref
):
    rhs, tile = base_ref.shape
    size = rhs * tile // LANES
    total = summed(received_ref)
    gram = unpack_sums(total[size:, :], 5 * rhs)
    half_wy, bb, yb, yy, wy = (gram[:, index * rhs : (index + 1) * rhs] for index in range(5))
    wy = wy + (half_wy + half_wy.T)
    curvature = yb + SHIFT * bb
    (inverse_curvature, inverse_bb), eye = inverses([curvature, bb])
    step_t = times(bb, inverse_curvature)
    step = times(inverse_curvature, bb)
    a1, a1_t = eye - SHIFT * step_t, eye - SHIFT * step
    b1, b1_t = -step_t, -step

    def inner(a, a_t, b, b_t, first, cross, last):
        return times(times(a, first) + times(b, cross), a_t) + times(
            times(a, cross) + times(b, last), b_t
        )

    next_gram = inner(a1, a1_t, b1, b1_t, bb, yb, yy)
    a2 = a1 + times(next_gram, inverse_bb)
    a2_t = a1_t + times(inverse_bb, next_gram)
    curvature = inner(a2, a2_t, b1, b1_t, yb + SHIFT * bb, yy + SHIFT * yb, wy + SHIFT * yy)
    (inverse_curvature,), eye = inverses([curvature])
    last_t = times(next_gram, inverse_curvature)
    base, mid = base_ref[...], mid_ref[...]
    top = from_tiles(total[:size, :], rhs) + shifted_ref[...] * mid
    from_mid = times(last_t, b1)
    from_base = times(last_t, a2)
    solution_ref[...] = times(step_t + from_base, base) + times(from_mid, mid)
    residual_ref[...] = (
        times(a1 - SHIFT * from_base, base)
        + times(b1 - from_base - SHIFT * from_mid, mid)
        - times(from_mid, top)
    )


def local(kernel_codes, tile_scales, kernel_diagonal, noise_variance, targets):
    rhs, tile = targets.shape
    slots = kernel_codes.shape[0] // (tile // 2)
    width = tile // LANES
    size = rhs * width
    row_count = lax.axis_size("row")
    col_count = lax.axis_size("col")
    side = slots * slots
    planes = col_count // side
    row_index = lax.axis_index("row")
    col_index = lax.axis_index("col")
    plane, spot = col_index // side, col_index % side
    place = jnp.stack(
        [
            col_index - row_index * slots,
            row_index,
            plane,
            spot // slots,
            spot,
            row_index // (row_count // planes),
            plane * (row_count // planes) + spot // slots,
            row_index % (row_count // planes),
        ]
    ).astype(jnp.int32)
    near = [[first * side + index for index in range(side)] for first in range(planes)]
    deep = [
        [row * col_count + first * side + index for first in range(planes) for row in range(row_count)]
        for index in range(side)
    ]
    deep_count = planes * row_count
    shifted = (lax.reduce_precision(kernel_diagonal, 8, 7) + (noise_variance - SHIFT))[None, :]

    def exchange_near(values):
        return lax.all_to_all(values, "col", 0, 0, axis_index_groups=near)

    def exchange_deep(values):
        return lax.all_to_all(values, ("row", "col"), 0, 0, axis_index_groups=deep)

    def exchange_row(values):
        return lax.all_to_all(values, "row", 0, 0)

    scales = tile_scales.T
    out_shape = (slots, slots, size + width, LANES)
    in_vmem = pltpu.VMEM(kernel_codes.shape, BF16)
    slabs, stored, outgoing, extra, scaled = pl.pallas_call(
        first_rows_kernel,
        in_specs=[SMEM, pl.BlockSpec(memory_space=pltpu.HBM)]
        + [pl.BlockSpec(memory_space=pltpu.VMEM)] * 3,
        out_specs=[pl.BlockSpec(memory_space=pltpu.VMEM), pl.BlockSpec(memory_space=pltpu.HBM)]
        + [pl.BlockSpec(memory_space=pltpu.VMEM)] * 3,
        out_shape=[in_vmem, pltpu.HBM(kernel_codes.shape, BF16), struct(out_shape, BF16)]
        + [struct((rhs, tile), F32)] * 2,
        scratch_shapes=[
            pltpu.VMEM((tile_scales.shape[0], tile), F32),
            pltpu.VMEM(kernel_codes.shape, BF16),
            pltpu.SemaphoreType.DMA((slots,)),
            pltpu.SemaphoreType.DMA((slots,)),
        ],
        compiler_params=PARAMS,
        name="first_rows",
    )(place, in_hbm(kernel_codes), scales, in_hbm(targets), shifted)
    received = exchange_near(outgoing.reshape(side, size + width, LANES))
    relayed = plain(
        functools.partial(relay_kernel, width),
        struct((deep_count, (slots + 1) * width, LANES), BF16),
        "relay",
        received,
        scalars=False,
    )
    received = exchange_deep(relayed)
    message = plain(
        first_own_kernel,
        struct((row_count, size + width, LANES), BF16),
        "first_own",
        place,
        in_place(slabs),
        received,
        targets,
        extra,
        scratch=[pltpu.VMEM((rhs, tile), F32), pltpu.VMEM((rhs, slots * tile), BF16)],
    )
    received = exchange_row(message)
    mid, own, outgoing = plain(
        combine_kernel,
        [struct((rhs, tile), F32), struct((rhs, tile), BF16), struct((side, width, LANES), BF16)],
        "combine",
        place,
        received,
        scaled,
    )
    received = exchange_near(outgoing)
    fetched = [pltpu.VMEM(kernel_codes.shape, BF16), pltpu.SemaphoreType.DMA((slots,))]
    sent, extra, grams = plain(
        functools.partial(second_rows_kernel, row_count),
        [
            struct((slots, rhs, tile), BF16),
            struct((rhs, tile), F32),
            struct((rhs, LANES), F32),
        ],
        "second_rows",
        place,
        in_hbm(stored),
        own,
        targets,
        mid,
        shifted,
        scratch=fetched,
        in_memory=(1,),
    )
    relayed = plain(
        spread_kernel,
        struct((deep_count, slots * width, LANES), BF16),
        "spread",
        received,
        scalars=False,
    )
    received = exchange_deep(relayed)
    outgoing, rows = pl.pallas_call(
        pair_kernel,
        in_specs=[SMEM] + [pl.BlockSpec(memory_space=pltpu.VMEM)] * 5,
        out_shape=[
            struct((side, size + rhs, LANES), BF16),
            struct((rhs, slots * tile), BF16),
        ],
        scratch_shapes=[pltpu.VMEM((rhs, LANES), F32)],
        compiler_params=PARAMS,
        name="pair",
    )(place, received, own, extra, sent, grams)
    received = exchange_near(outgoing)
    total = plain(
        second_own_kernel,
        struct((size, LANES), F32),
        "second_own",
        place,
        in_hbm(stored),
        rows,
        own,
        extra,
        scratch=[pltpu.VMEM((rhs, tile), F32), *fetched],
        in_memory=(1,),
    )
    outgoing = plain(
        join_kernel,
        struct((deep_count, size + rhs, LANES), BF16),
        "join",
        place,
        received,
        total,
    )
    received = exchange_deep(outgoing)
    return tuple(
        plain(
            final_kernel,
            [struct((rhs, tile), F32)] * 2,
            "small_solves",
            received,
            targets,
            mid,
            shifted,
            scalars=False,
        )
    )


def solution(mesh):
    in_specs = (P("row", "col"), P("row", "col"), P("col"), P("col"), P(None, "col"))
    out_specs = (P(None, "col"), P(None, "col"))
    return jax.shard_map(local, mesh=mesh, in_specs=in_specs, out_specs=out_specs, check_vma=False)
```

```python
import functools

import jax
import jax.numpy as jnp
from jax import lax
from jax.experimental import pallas as pl
from jax.experimental.pallas import tpu as pltpu
from jax.sharding import PartitionSpec as P

F32 = jnp.float32
BF16 = jnp.bfloat16
SHIFT = 3.0
STORED_FIRST = 2
VMEM_LIMIT = 32 * 1024 * 1024


def spread_scales(scales_ref, wide_ref):
    col_blocks = scales_ref.shape[0]
    cols = wide_ref.shape[1]
    lane_block = lax.broadcasted_iota(jnp.int32, (col_blocks, cols), 1) // (cols // col_blocks)
    own_block = lax.broadcasted_iota(jnp.int32, (col_blocks, cols), 0)
    spread = jnp.where(lane_block == own_block, 1.0, 0.0).astype(F32)
    wide_ref[...] = lax.dot_general(
        scales_ref[...],
        spread,
        (((0,), (0,)), ((), ())),
        precision=lax.Precision.HIGHEST,
        preferred_element_type=F32,
    )


def dequantize_slot(slot, slots, codes_ref, wide_ref, slab_ref, copies=()):
    rows = codes_ref.shape[0] // slots
    block_rows = wide_ref.shape[0] // slots
    order = rows // block_rows
    for index, block in enumerate(range(slot * block_rows, (slot + 1) * block_rows)):
        if copies and index % (block_rows // len(copies)) == 0:
            copies[index // (block_rows // len(copies))].wait()
        part = slice(block * order, (block + 1) * order)
        wide = wide_ref[block : block + 1, :]
        slab_ref[part, :] = (codes_ref[part, :].astype(F32) * wide).astype(BF16)


NT = (((1,), (1,)), ((), ()))


def dot(left, right):
    return jnp.dot(left, right, preferred_element_type=F32)


def dot_t(left, right):
    return lax.dot_general(left, right, NT, preferred_element_type=F32)


def triangles(slab_ref):
    half = slab_ref.shape[0]
    mixed = slab_ref[:, :half]
    row = lax.broadcasted_iota(jnp.int32, (half, half), 0)
    col = lax.broadcasted_iota(jnp.int32, (half, half), 1)
    zero = jnp.zeros_like(mixed)
    return jnp.where(row > col, mixed, zero), jnp.where(row < col, mixed, zero)


LANES = 128


def to_tiles(values):
    count = values.shape[1] // LANES
    return jnp.concatenate(
        [values[:, part * LANES : (part + 1) * LANES] for part in range(count)], axis=0
    )


def from_tiles(tiles, rhs):
    count = tiles.shape[0] // rhs
    return jnp.concatenate(
        [tiles[part * rhs : (part + 1) * rhs, :] for part in range(count)], axis=1
    )


def row_tiles(values):
    return values.reshape(values.shape[0], values.shape[1] // LANES, LANES)


def flat_rows(tiles):
    return tiles.reshape(tiles.shape[0], tiles.shape[1] * LANES)


def share_of(values, row_index):
    tiles = row_tiles(values)
    row = lax.broadcasted_iota(jnp.int32, tiles.shape, 0)
    return jnp.sum(jnp.where(row == row_index, tiles, 0.0), axis=0)


def toward_rows(slot, offset, slab_ref, own, put, extra_ref, beside):
    half, tile = slab_ref.shape
    rhs = own.shape[0]

    @pl.when(slot < offset)
    def _():
        second = dot_t(own, slab_ref[...])
        beside()
        put(jnp.concatenate([second, jnp.zeros((rhs, tile - half), F32)], axis=1))

    @pl.when(slot > offset)
    def _():
        first = dot(own[:, half:], slab_ref[...])
        beside()
        put(first)

    @pl.when(slot == offset)
    def _():
        low, high = triangles(slab_ref)
        head, tail = own[:, :half], own[:, half:]
        extra_ref[:, :half] = dot_t(head, low) + dot_t(tail, slab_ref[:, half:])
        extra_ref[:, half:] = dot_t(tail, high)
        beside()
        put(jnp.zeros((rhs, tile), F32))


def slot_copies(source_ref, target_ref, semaphores, first=0, last=None):
    slots = semaphores.shape[0]
    half = source_ref.shape[0] // slots
    copies = []
    for slot in range(first, slots if last is None else last):
        part = pl.ds(slot * half, half)
        copies.append(
            pltpu.make_async_copy(
                source_ref.at[part, :], target_ref.at[part, :], semaphores.at[slot]
            )
        )
    return copies


def slot_of(slab_ref, slot, half):
    return slab_ref.at[pl.ds(slot * half, half), :]


def first_rows_kernel(
    place_ref,
    codes_hbm,
    scales_hbm,
    base_hbm,
    diagonal_hbm,
    noise_hbm,
    slab_ref,
    stored_hbm,
    out_ref,
    extra_ref,
    scaled_ref,
    shifted_ref,
    wide_ref,
    codes_ref,
    scales_ref,
    base_ref,
    points_ref,
    arrived,
    stored,
    small,
):
    slots = out_ref.shape[1]
    half = slab_ref.shape[0] // slots
    sources = (scales_hbm, base_hbm, diagonal_hbm, noise_hbm)
    targets = (scales_ref, base_ref, points_ref.at[0], points_ref.at[1])
    inputs = [
        pltpu.make_async_copy(source, target, small.at[index])
        for index, (source, target) in enumerate(zip(sources, targets))
    ]
    copies = slot_copies(codes_hbm, codes_ref, arrived)
    stores = slot_copies(slab_ref, stored_hbm, stored, last=STORED_FIRST)
    each = len(copies) // slots
    for copy in inputs[:1] + copies[:each] + inputs[1:] + copies[each:]:
        copy.start()
    rhs, tile = base_ref.shape
    size = rhs * tile // LANES
    inputs[0].wait()
    spread_scales(scales_ref, wide_ref)
    extra_ref[...] = jnp.zeros_like(extra_ref)
    dequantize_slot(0, slots, codes_ref, wide_ref, slab_ref, copies[:each])
    stores[0].start()
    inputs[1].wait()
    own = base_ref[...].astype(BF16)
    for slot in range(slots):
        for copy in copies[(slot + 1) * each : (slot + 2) * each]:
            copy.wait()

        def beside(slot=slot):
            if slot + 1 < slots:
                dequantize_slot(slot + 1, slots, codes_ref, wide_ref, slab_ref)

        def put(values, slot=slot):
            tiles = to_tiles(values).astype(BF16)
            for copy in range(slots):
                out_ref[copy, slot, :size, :] = tiles

        view = slot_of(slab_ref, slot, half)
        toward_rows(slot, place_ref[0], view, own, put, extra_ref, beside)
        if slot + 1 < len(stores):
            stores[slot + 1].start()
    for copy in inputs[2:]:
        copy.wait()
    base = base_ref[...]
    shifted = points_ref[0:1, :].astype(BF16).astype(F32) + (points_ref[1:2, :] - SHIFT)
    shifted_ref[...] = shifted
    scaled_ref[...] = shifted * base
    share = share_of(base, place_ref[1]).astype(BF16)
    for copy in range(slots):
        for slot in range(slots):
            out_ref[copy, slot, size:, :] = share
    for store in stores:
        store.wait()


def second_rows_kernel(
    copies, place_ref, slab_hbm, own_ref, base_ref, mid_ref, shifted_ref,
    out_ref, extra_ref, sums_ref, slab_ref, arrived
):
    fetches = slot_copies(slab_hbm, slab_ref, arrived)
    for fetch in fetches:
        fetch.start()
    rhs = own_ref.shape[0]
    base, mid = base_ref[...], mid_ref[...]
    exact = functools.partial(
        lax.dot_general,
        dimension_numbers=NT,
        precision=lax.Precision.HIGHEST,
        preferred_element_type=F32,
    )
    on_base = exact(jnp.concatenate([base, mid]), base)
    on_mid = exact(jnp.concatenate([mid, shifted_ref[...] * mid]), mid)
    sums_ref[...] = jnp.zeros_like(sums_ref)
    for part, value in enumerate((on_base[:rhs], on_base[rhs:], on_mid[:rhs], on_mid[rhs:])):
        sums_ref[:, (part + 1) * rhs : (part + 2) * rhs] = value * (1.0 / copies)
    extra_ref[...] = jnp.zeros_like(extra_ref)
    for slot in range(out_ref.shape[0]):

        def put(values, slot=slot):
            out_ref[slot, :, :] = values.astype(BF16)

        half = slab_ref.shape[0] // out_ref.shape[0]
        view = slot_of(slab_ref, slot, half)
        fetches[slot].wait()
        toward_rows(slot, place_ref[0], view, own_ref[...], put, extra_ref, lambda: None)


def relay_kernel(width, received_ref, out_ref):
    senders, height, lanes = received_ref.shape
    copies, full, lanes = out_ref.shape
    size = height - width
    slots = full // width - 1
    rhs = size // width
    reduced = received_ref[0, :size, :].astype(F32)
    for sender in range(1, senders):
        reduced = reduced + received_ref[sender, :size, :].astype(F32)
    rows = row_tiles(from_tiles(reduced, rhs)).astype(BF16)
    groups = []
    for first in range(0, senders, slots):
        pieces = [received_ref[first + part, size:, :].astype(F32) for part in range(slots)]
        groups.append(jnp.concatenate(pieces, axis=0).astype(BF16))
    for copy in range(copies):
        out_ref[copy, : slots * width, :] = groups[copy % len(groups)]
        out_ref[copy, slots * width :, :] = rows[copy % rhs]


def spread_kernel(received_ref, out_ref):
    senders, width, lanes = received_ref.shape
    slots = out_ref.shape[1] // width
    for first in range(0, senders, slots):
        pieces = [received_ref[first + part].astype(F32) for part in range(slots)]
        group = jnp.concatenate(pieces, axis=0).astype(BF16)
        for copy in range(first // slots, out_ref.shape[0], senders // slots):
            out_ref[copy, :, :] = group


def gather_rows(place_ref, received_ref, rows_ref, tile, slots):
    rhs = rows_ref.shape[0]
    start = place_ref[5] * rhs
    size = slots * tile // LANES
    piece = received_ref[pl.ds(start, rhs), :size, :].astype(F32)
    rows_ref[...] = flat_rows(piece).astype(BF16)


def toward_own(slot, offset, slab_ref, rows_ref, own, total_ref):
    half, tile = slab_ref.shape
    lanes = pl.multiple_of(slot * tile, tile)

    @pl.when(slot < offset)
    def _():
        total_ref[...] += dot(rows_ref[:, pl.ds(lanes, half)], slab_ref[...])

    @pl.when(slot > offset)
    def _():
        total_ref[:, half:] += dot_t(rows_ref[:, pl.ds(lanes, tile)], slab_ref[...])

    @pl.when(slot == offset)
    def _():
        low, high = triangles(slab_ref)
        head, tail = own[:, :half], own[:, half:]
        total_ref[:, :half] += dot(head, low)
        total_ref[:, half:] += dot(head, slab_ref[:, half:]) + dot(tail, high)


def all_toward_own(place_ref, slab_ref, rows_ref, own, total_ref, fetches=None):
    slots = rows_ref.shape[1] // own.shape[1]
    half = slab_ref.shape[0] // slots
    for slot in range(slots):
        if fetches is not None:
            fetches[slot].wait()
        toward_own(slot, place_ref[0], slot_of(slab_ref, slot, half), rows_ref, own, total_ref)


def first_own_kernel(
    place_ref, slab_ref, received_ref, base_ref, extra_ref, begun_hbm,
    out_ref, stored_hbm, total_ref, rows_ref, stored
):
    stores = slot_copies(slab_ref, stored_hbm, stored, first=STORED_FIRST)
    for store in stores:
        store.start()
    rhs, tile = base_ref.shape
    slots = rows_ref.shape[1] // tile
    width = tile // LANES
    total_ref[...] = extra_ref[...]
    gather_rows(place_ref, received_ref, rows_ref, tile, slots)
    all_toward_own(place_ref, slab_ref, rows_ref, base_ref[...].astype(BF16), total_ref)
    size = rhs * tile // LANES
    source = place_ref[6]
    planes = received_ref.shape[0] // rhs
    part = slice(slots * width, (slots + 1) * width)
    reduced = received_ref[source, part, :].astype(F32)
    for plane in range(1, planes):
        reduced = reduced + received_ref[plane * rhs + source, part, :].astype(F32)
    reduced = reduced.astype(BF16)
    tiles = to_tiles(total_ref[...]).astype(BF16)
    for copy in range(out_ref.shape[0]):
        out_ref[copy, :size, :] = tiles
        out_ref[copy, size:, :] = reduced
    for store in stores:
        store.wait()


def combine_kernel(place_ref, received_ref, scaled_ref, mid_ref, own_ref, out_ref):
    rhs, tile = scaled_ref.shape
    size = rhs * tile // LANES
    total = received_ref[0, :size, :].astype(F32)
    for sender in range(1, received_ref.shape[0]):
        total = total + received_ref[sender, :size, :].astype(F32)
    others = flat_rows(received_ref[:, size:, :].astype(F32))
    mid = (from_tiles(total, rhs) + others) + scaled_ref[...]
    mid_ref[...] = mid
    own_ref[...] = mid.astype(BF16)
    share = share_of(mid, place_ref[1]).astype(BF16)
    for copy in range(out_ref.shape[0]):
        out_ref[copy, :, :] = share


def three_parts(values):
    first = values.astype(BF16).astype(F32)
    rest = values - first
    second = rest.astype(BF16).astype(F32)
    return first, second, rest - second


def pack_sums(values, used):
    parts = [part[:, :used] for part in three_parts(values)]
    blank = jnp.zeros((values.shape[0], LANES - 3 * used), F32)
    return jnp.concatenate(parts + [blank], axis=1).astype(BF16)


def unpack_sums(values, used):
    return (values[:, :used] + values[:, used : 2 * used]) + values[:, 2 * used : 3 * used]


def pair_kernel(
    place_ref, received_ref, own_ref, extra_ref, sent_ref, grams_ref, out_ref, rows_ref, sums_ref
):
    rhs, tile = own_ref.shape
    slots = sent_ref.shape[0]
    size = rhs * tile // LANES
    gather_rows(place_ref, received_ref, rows_ref, tile, slots)
    pair = dot_t(extra_ref[...].astype(BF16), own_ref[...])
    for part in range(slots):
        pair = pair + dot_t(sent_ref[part], rows_ref[:, part * tile : (part + 1) * tile])
    sums_ref[...] = grams_ref[...]
    sums_ref[:, :rhs] = pair
    packed = pack_sums(sums_ref[...], 5 * rhs)
    for target in range(out_ref.shape[0]):
        out_ref[target, size:, :] = packed
    for part in range(slots):
        tiles = to_tiles(sent_ref[part].astype(F32)).astype(BF16)
        for target in range(part, out_ref.shape[0], slots):
            out_ref[target, :size, :] = tiles


def second_own_kernel(
    place_ref, slab_hbm, rows_ref, own_ref, extra_ref, out_ref, total_ref, slab_ref, arrived
):
    fetches = slot_copies(slab_hbm, slab_ref, arrived)
    for fetch in fetches:
        fetch.start()
    total_ref[...] = extra_ref[...]
    all_toward_own(place_ref, slab_ref, rows_ref, own_ref[...], total_ref, fetches)
    out_ref[...] = to_tiles(total_ref[...])


def summed(received_ref):
    total = received_ref[0, :, :].astype(F32)
    for sender in range(1, received_ref.shape[0]):
        total = total + received_ref[sender, :, :].astype(F32)
    return total


def join_kernel(place_ref, received_ref, own_ref, out_ref):
    size, lanes = own_ref.shape
    rhs = out_ref.shape[1] - size
    total = summed(received_ref)
    packed = pack_sums(unpack_sums(total[size:, :], 5 * rhs), 5 * rhs)
    planes = out_ref.shape[0] // rhs
    for plane in range(planes):
        for_own = place_ref[2] == plane
        for_row = jnp.logical_and(place_ref[5] == plane, place_ref[3] == place_ref[7])
        value = jnp.where(for_own, own_ref[...], 0.0) + jnp.where(for_row, total[:size, :], 0.0)
        value = value.astype(BF16)
        for copy in range(rhs):
            out_ref[plane * rhs + copy, :size, :] = value
            out_ref[plane * rhs + copy, size:, :] = packed


SMEM = pl.BlockSpec(memory_space=pltpu.SMEM)
PARAMS = pltpu.CompilerParams(vmem_limit_bytes=VMEM_LIMIT)


def struct(shape, dtype):
    return jax.ShapeDtypeStruct(shape, dtype)


def in_place(values):
    return pltpu.with_memory_space_constraint(values, pltpu.VMEM)


def in_hbm(values):
    return pltpu.with_memory_space_constraint(values, pltpu.HBM)


def plain(kernel, outs, name, *operands, scalars=True, scratch=(), in_memory=()):
    specs = [pl.BlockSpec(memory_space=pltpu.VMEM)] * len(operands)
    if scalars:
        specs[0] = SMEM
    for index in in_memory:
        specs[index] = pl.BlockSpec(memory_space=pltpu.HBM)
    return pl.pallas_call(
        kernel,
        in_specs=specs,
        out_shape=outs,
        scratch_shapes=scratch,
        compiler_params=PARAMS,
        name=name,
    )(*operands)


def times(left, right):
    total = left[:, 0:1] * right[0:1, :]
    for index in range(1, left.shape[1]):
        total = total + left[:, index : index + 1] * right[index : index + 1, :]
    return total


def inverses(matrices):
    size = matrices[0].shape[0]
    row = lax.broadcasted_iota(jnp.int32, (size, size), 0)
    col = lax.broadcasted_iota(jnp.int32, (size, size), 1)
    eye = jnp.where(row == col, 1.0, 0.0).astype(F32)
    work = [(matrix, eye) for matrix in matrices]
    for step in range(size):
        here = row == step
        following = []
        for left, right in work:
            scale = 1.0 / left[step : step + 1, step : step + 1]
            left_row = left[step : step + 1, :] * scale
            right_row = right[step : step + 1, :] * scale
            column = left[:, step : step + 1]
            following.append(
                (
                    jnp.where(here, left_row, left - column * left_row),
                    jnp.where(here, right_row, right - column * right_row),
                )
            )
        work = following
    return [right for left, right in work], eye


def final_kernel(
    received_ref, base_ref, mid_ref, shifted_ref, solution_ref, residual_ref
):
    rhs, tile = base_ref.shape
    size = rhs * tile // LANES
    total = summed(received_ref)
    gram = unpack_sums(total[size:, :], 5 * rhs)
    half_wy, bb, yb, yy, wy = (gram[:, index * rhs : (index + 1) * rhs] for index in range(5))
    wy = wy + (half_wy + half_wy.T)
    curvature = yb + SHIFT * bb
    (inverse_curvature, inverse_bb), eye = inverses([curvature, bb])
    step_t = times(bb, inverse_curvature)
    step = times(inverse_curvature, bb)
    a1, a1_t = eye - SHIFT * step_t, eye - SHIFT * step
    b1, b1_t = -step_t, -step

    def inner(a, a_t, b, b_t, first, cross, last):
        return times(times(a, first) + times(b, cross), a_t) + times(
            times(a, cross) + times(b, last), b_t
        )

    next_gram = inner(a1, a1_t, b1, b1_t, bb, yb, yy)
    a2 = a1 + times(next_gram, inverse_bb)
    a2_t = a1_t + times(inverse_bb, next_gram)
    curvature = inner(a2, a2_t, b1, b1_t, yb + SHIFT * bb, yy + SHIFT * yb, wy + SHIFT * yy)
    (inverse_curvature,), eye = inverses([curvature])
    last_t = times(next_gram, inverse_curvature)
    base, mid = base_ref[...], mid_ref[...]
    top = from_tiles(total[:size, :], rhs) + shifted_ref[...] * mid
    from_mid = times(last_t, b1)
    from_base = times(last_t, a2)
    solution_ref[...] = times(step_t + from_base, base) + times(from_mid, mid)
    residual_ref[...] = (
        times(a1 - SHIFT * from_base, base)
        + times(b1 - from_base - SHIFT * from_mid, mid)
        - times(from_mid, top)
    )


def local(kernel_codes, tile_scales, kernel_diagonal, noise_variance, targets):
    rhs, tile = targets.shape
    slots = kernel_codes.shape[0] // (tile // 2)
    width = tile // LANES
    size = rhs * width
    row_count = lax.axis_size("row")
    col_count = lax.axis_size("col")
    side = slots * slots
    planes = col_count // side
    row_index = lax.axis_index("row")
    col_index = lax.axis_index("col")
    plane, spot = col_index // side, col_index % side
    place = jnp.stack(
        [
            col_index - row_index * slots,
            row_index,
            plane,
            spot // slots,
            spot,
            row_index // (row_count // planes),
            plane * (row_count // planes) + spot // slots,
            row_index % (row_count // planes),
        ]
    ).astype(jnp.int32)
    near = [[first * side + index for index in range(side)] for first in range(planes)]
    deep = [
        [row * col_count + first * side + index for first in range(planes) for row in range(row_count)]
        for index in range(side)
    ]
    deep_count = planes * row_count

    def exchange_near(values):
        return lax.all_to_all(values, "col", 0, 0, axis_index_groups=near)

    def exchange_deep(values):
        return lax.all_to_all(values, ("row", "col"), 0, 0, axis_index_groups=deep)

    def exchange_row(values):
        return lax.all_to_all(values, "row", 0, 0)

    scales = tile_scales.T
    out_shape = (slots, slots, size + width, LANES)
    in_vmem = pltpu.VMEM(kernel_codes.shape, BF16)
    small = len((scales, targets, kernel_diagonal, noise_variance))
    slabs, stored, outgoing, extra, scaled, shifted = pl.pallas_call(
        first_rows_kernel,
        in_specs=[SMEM] + [pl.BlockSpec(memory_space=pltpu.HBM)] * 5,
        out_specs=[pl.BlockSpec(memory_space=pltpu.VMEM), pl.BlockSpec(memory_space=pltpu.HBM)]
        + [pl.BlockSpec(memory_space=pltpu.VMEM)] * 4,
        out_shape=[in_vmem, pltpu.HBM(kernel_codes.shape, BF16), struct(out_shape, BF16)]
        + [struct((rhs, tile), F32)] * 2
        + [struct((1, tile), F32)],
        scratch_shapes=[
            pltpu.VMEM((tile_scales.shape[0], tile), F32),
            pltpu.VMEM(kernel_codes.shape, BF16),
            pltpu.VMEM(scales.shape, F32),
            pltpu.VMEM(targets.shape, F32),
            pltpu.VMEM((2, tile), F32),
            pltpu.SemaphoreType.DMA((4 * slots,)),
            pltpu.SemaphoreType.DMA((slots,)),
            pltpu.SemaphoreType.DMA((small,)),
        ],
        compiler_params=PARAMS,
        name="first_rows",
    )(
        place,
        in_hbm(kernel_codes),
        in_hbm(scales),
        in_hbm(targets),
        in_hbm(kernel_diagonal),
        in_hbm(noise_variance),
    )
    received = exchange_near(outgoing.reshape(side, size + width, LANES))
    relayed = plain(
        functools.partial(relay_kernel, width),
        struct((deep_count, (slots + 1) * width, LANES), BF16),
        "relay",
        received,
        scalars=False,
    )
    received = exchange_deep(relayed)
    vmem, hbm = pl.BlockSpec(memory_space=pltpu.VMEM), pl.BlockSpec(memory_space=pltpu.HBM)
    message, stored = pl.pallas_call(
        first_own_kernel,
        in_specs=[SMEM] + [vmem] * 4 + [hbm],
        out_specs=[vmem, hbm],
        out_shape=[
            struct((row_count, size + width, LANES), BF16),
            pltpu.HBM(kernel_codes.shape, BF16),
        ],
        scratch_shapes=[
            pltpu.VMEM((rhs, tile), F32),
            pltpu.VMEM((rhs, slots * tile), BF16),
            pltpu.SemaphoreType.DMA((slots,)),
        ],
        input_output_aliases={5: 1},
        compiler_params=PARAMS,
        name="first_own",
    )(place, in_place(slabs), received, targets, extra, in_hbm(stored))
    received = exchange_row(message)
    mid, own, outgoing = plain(
        combine_kernel,
        [struct((rhs, tile), F32), struct((rhs, tile), BF16), struct((side, width, LANES), BF16)],
        "combine",
        place,
        received,
        scaled,
    )
    received = exchange_near(outgoing)
    fetched = [pltpu.VMEM(kernel_codes.shape, BF16), pltpu.SemaphoreType.DMA((slots,))]
    sent, extra, grams = plain(
        functools.partial(second_rows_kernel, row_count),
        [
            struct((slots, rhs, tile), BF16),
            struct((rhs, tile), F32),
            struct((rhs, LANES), F32),
        ],
        "second_rows",
        place,
        in_hbm(stored),
        own,
        targets,
        mid,
        shifted,
        scratch=fetched,
        in_memory=(1,),
    )
    relayed = plain(
        spread_kernel,
        struct((deep_count, slots * width, LANES), BF16),
        "spread",
        received,
        scalars=False,
    )
    received = exchange_deep(relayed)
    outgoing, rows = pl.pallas_call(
        pair_kernel,
        in_specs=[SMEM] + [pl.BlockSpec(memory_space=pltpu.VMEM)] * 5,
        out_shape=[
            struct((side, size + rhs, LANES), BF16),
            struct((rhs, slots * tile), BF16),
        ],
        scratch_shapes=[pltpu.VMEM((rhs, LANES), F32)],
        compiler_params=PARAMS,
        name="pair",
    )(place, received, own, extra, sent, grams)
    received = exchange_near(outgoing)
    total = plain(
        second_own_kernel,
        struct((size, LANES), F32),
        "second_own",
        place,
        in_hbm(stored),
        rows,
        own,
        extra,
        scratch=[pltpu.VMEM((rhs, tile), F32), *fetched],
        in_memory=(1,),
    )
    outgoing = plain(
        join_kernel,
        struct((deep_count, size + rhs, LANES), BF16),
        "join",
        place,
        received,
        total,
    )
    received = exchange_deep(outgoing)
    return tuple(
        plain(
            final_kernel,
            [struct((rhs, tile), F32)] * 2,
            "small_solves",
            received,
            targets,
            mid,
            shifted,
            scalars=False,
        )
    )


def solution(mesh):
    in_specs = (P("row", "col"), P("row", "col"), P("col"), P("col"), P(None, "col"))
    out_specs = (P(None, "col"), P(None, "col"))
    return jax.shard_map(local, mesh=mesh, in_specs=in_specs, out_specs=out_specs, check_vma=False)
```

```python
import functools

import jax
import jax.numpy as jnp
from jax import lax
from jax.experimental import pallas as pl
from jax.experimental.pallas import tpu as pltpu
from jax.sharding import PartitionSpec as P

F32 = jnp.float32
BF16 = jnp.bfloat16
SHIFT = 3.0
STORED_FIRST = 2
VMEM_LIMIT = 32 * 1024 * 1024


def spread_scales(scales_ref, wide_ref):
    col_blocks = scales_ref.shape[0]
    cols = wide_ref.shape[1]
    lane_block = lax.broadcasted_iota(jnp.int32, (col_blocks, cols), 1) // (cols // col_blocks)
    own_block = lax.broadcasted_iota(jnp.int32, (col_blocks, cols), 0)
    spread = jnp.where(lane_block == own_block, 1.0, 0.0).astype(BF16)
    parts = jnp.concatenate(three_parts(scales_ref[...]), axis=1).astype(BF16)
    wide = lax.dot_general(
        parts, spread, (((0,), (0,)), ((), ())), preferred_element_type=F32
    )
    count = wide_ref.shape[0]
    wide_ref[...] = wide[:count] + (wide[count : 2 * count] + wide[2 * count :])


def dequantize_slot(slot, slots, codes_ref, wide_ref, slab_ref, copies=()):
    rows = codes_ref.shape[0] // slots
    block_rows = wide_ref.shape[0] // slots
    order = rows // block_rows
    for index, block in enumerate(range(slot * block_rows, (slot + 1) * block_rows)):
        if copies and index % (block_rows // len(copies)) == 0:
            copies[index // (block_rows // len(copies))].wait()
        part = slice(block * order, (block + 1) * order)
        wide = wide_ref[block : block + 1, :]
        slab_ref[part, :] = (codes_ref[part, :].astype(F32) * wide).astype(BF16)


NT = (((1,), (1,)), ((), ()))


def dot(left, right):
    return jnp.dot(left, right, preferred_element_type=F32)


def dot_t(left, right):
    return lax.dot_general(left, right, NT, preferred_element_type=F32)


def triangles(slab_ref):
    half = slab_ref.shape[0]
    mixed = slab_ref[:, :half]
    row = lax.broadcasted_iota(jnp.int32, (half, half), 0)
    col = lax.broadcasted_iota(jnp.int32, (half, half), 1)
    zero = jnp.zeros_like(mixed)
    return jnp.where(row > col, mixed, zero), jnp.where(row < col, mixed, zero)


LANES = 128


def to_tiles(values):
    count = values.shape[1] // LANES
    return jnp.concatenate(
        [values[:, part * LANES : (part + 1) * LANES] for part in range(count)], axis=0
    )


def from_tiles(tiles, rhs):
    count = tiles.shape[0] // rhs
    return jnp.concatenate(
        [tiles[part * rhs : (part + 1) * rhs, :] for part in range(count)], axis=1
    )


def row_tiles(values):
    return values.reshape(values.shape[0], values.shape[1] // LANES, LANES)


def flat_rows(tiles):
    return tiles.reshape(tiles.shape[0], tiles.shape[1] * LANES)


def share_of(values, row_index):
    tiles = row_tiles(values)
    row = lax.broadcasted_iota(jnp.int32, tiles.shape, 0)
    return jnp.sum(jnp.where(row == row_index, tiles, 0.0), axis=0)


def toward_rows(slot, offset, slab_ref, own, put, extra_ref, beside):
    half, tile = slab_ref.shape
    rhs = own.shape[0]

    @pl.when(slot < offset)
    def _():
        beside()
        second = dot_t(own, slab_ref[...])
        put(jnp.concatenate([second, jnp.zeros((rhs, tile - half), F32)], axis=1))

    @pl.when(slot > offset)
    def _():
        beside()
        first = dot(own[:, half:], slab_ref[...])
        put(first)

    @pl.when(slot == offset)
    def _():
        low, high = triangles(slab_ref)
        head, tail = own[:, :half], own[:, half:]
        extra_ref[:, :half] = dot_t(head, low) + dot_t(tail, slab_ref[:, half:])
        extra_ref[:, half:] = dot_t(tail, high)
        beside()
        put(jnp.zeros((rhs, tile), F32))


def slot_copies(source_ref, target_ref, semaphores, first=0, last=None):
    slots = semaphores.shape[0]
    half = source_ref.shape[0] // slots
    copies = []
    for slot in range(first, slots if last is None else last):
        part = pl.ds(slot * half, half)
        copies.append(
            pltpu.make_async_copy(
                source_ref.at[part, :], target_ref.at[part, :], semaphores.at[slot]
            )
        )
    return copies


def slot_of(slab_ref, slot, half):
    return slab_ref.at[pl.ds(slot * half, half), :]


def first_rows_kernel(
    place_ref,
    codes_hbm,
    scales_hbm,
    base_hbm,
    diagonal_hbm,
    noise_hbm,
    slab_ref,
    stored_hbm,
    out_ref,
    extra_ref,
    scaled_ref,
    shifted_ref,
    wide_ref,
    codes_ref,
    scales_ref,
    base_ref,
    points_ref,
    arrived,
    stored,
    small,
):
    slots = out_ref.shape[1]
    half = slab_ref.shape[0] // slots
    sources = (scales_hbm, base_hbm, diagonal_hbm, noise_hbm)
    targets = (scales_ref, base_ref, points_ref.at[0], points_ref.at[1])
    inputs = [
        pltpu.make_async_copy(source, target, small.at[index])
        for index, (source, target) in enumerate(zip(sources, targets))
    ]
    copies = slot_copies(codes_hbm, codes_ref, arrived)
    stores = slot_copies(slab_ref, stored_hbm, stored, last=STORED_FIRST)
    each = len(copies) // slots
    for copy in inputs[:1] + copies[:each] + inputs[1:] + copies[each:]:
        copy.start()
    rhs, tile = base_ref.shape
    size = rhs * tile // LANES
    inputs[0].wait()
    spread_scales(scales_ref, wide_ref)
    extra_ref[...] = jnp.zeros_like(extra_ref)
    dequantize_slot(0, slots, codes_ref, wide_ref, slab_ref, copies[:each])
    stores[0].start()
    inputs[1].wait()
    own = base_ref[...].astype(BF16)
    for slot in range(slots):
        for copy in copies[(slot + 1) * each : (slot + 2) * each]:
            copy.wait()

        def beside(slot=slot):
            if slot + 1 < slots:
                dequantize_slot(slot + 1, slots, codes_ref, wide_ref, slab_ref)

        def put(values, slot=slot):
            tiles = to_tiles(values).astype(BF16)
            for copy in range(slots):
                out_ref[copy, slot, :size, :] = tiles

        view = slot_of(slab_ref, slot, half)
        toward_rows(slot, place_ref[0], view, own, put, extra_ref, beside)
        if slot + 1 < len(stores):
            stores[slot + 1].start()
    for copy in inputs[2:]:
        copy.wait()
    base = base_ref[...]
    shifted = points_ref[0:1, :].astype(BF16).astype(F32) + (points_ref[1:2, :] - SHIFT)
    shifted_ref[...] = shifted
    scaled_ref[...] = shifted * base
    share = share_of(base, place_ref[1]).astype(BF16)
    for copy in range(slots):
        for slot in range(slots):
            out_ref[copy, slot, size:, :] = share
    for store in stores:
        store.wait()


def second_rows_kernel(
    copies, place_ref, slab_hbm, own_ref, base_ref, mid_ref, shifted_ref,
    out_ref, extra_ref, sums_ref, slab_ref, arrived
):
    fetches = slot_copies(slab_hbm, slab_ref, arrived)
    for fetch in fetches:
        fetch.start()
    rhs = own_ref.shape[0]
    base, mid = base_ref[...], mid_ref[...]
    exact = functools.partial(
        lax.dot_general,
        dimension_numbers=NT,
        precision=lax.Precision.HIGHEST,
        preferred_element_type=F32,
    )
    on_base = exact(jnp.concatenate([base, mid]), base)
    on_mid = exact(jnp.concatenate([mid, shifted_ref[...] * mid]), mid)
    sums_ref[...] = jnp.zeros_like(sums_ref)
    for part, value in enumerate((on_base[:rhs], on_base[rhs:], on_mid[:rhs], on_mid[rhs:])):
        sums_ref[:, (part + 1) * rhs : (part + 2) * rhs] = value * (1.0 / copies)
    extra_ref[...] = jnp.zeros_like(extra_ref)
    for slot in range(out_ref.shape[0]):

        def put(values, slot=slot):
            out_ref[slot, :, :] = values.astype(BF16)

        half = slab_ref.shape[0] // out_ref.shape[0]
        view = slot_of(slab_ref, slot, half)
        fetches[slot].wait()
        toward_rows(slot, place_ref[0], view, own_ref[...], put, extra_ref, lambda: None)


def relay_kernel(width, received_ref, out_ref):
    senders, height, lanes = received_ref.shape
    copies, full, lanes = out_ref.shape
    size = height - width
    slots = full // width - 1
    rhs = size // width
    reduced = received_ref[0, :size, :].astype(F32)
    for sender in range(1, senders):
        reduced = reduced + received_ref[sender, :size, :].astype(F32)
    rows = row_tiles(from_tiles(reduced, rhs)).astype(BF16)
    groups = []
    for first in range(0, senders, slots):
        pieces = [received_ref[first + part, size:, :].astype(F32) for part in range(slots)]
        groups.append(jnp.concatenate(pieces, axis=0).astype(BF16))
    for copy in range(copies):
        out_ref[copy, : slots * width, :] = groups[copy % len(groups)]
        out_ref[copy, slots * width :, :] = rows[copy % rhs]


def spread_kernel(received_ref, out_ref):
    senders, width, lanes = received_ref.shape
    slots = out_ref.shape[1] // width
    for first in range(0, senders, slots):
        pieces = [received_ref[first + part].astype(F32) for part in range(slots)]
        group = jnp.concatenate(pieces, axis=0).astype(BF16)
        for copy in range(first // slots, out_ref.shape[0], senders // slots):
            out_ref[copy, :, :] = group


def gather_rows(place_ref, received_ref, rows_ref, tile, slots):
    rhs = rows_ref.shape[0]
    start = place_ref[5] * rhs
    size = slots * tile // LANES
    piece = received_ref[pl.ds(start, rhs), :size, :].astype(F32)
    rows_ref[...] = flat_rows(piece).astype(BF16)


def toward_own(slot, offset, slab_ref, rows_ref, own, total_ref):
    half, tile = slab_ref.shape
    lanes = pl.multiple_of(slot * tile, tile)

    @pl.when(slot < offset)
    def _():
        total_ref[...] += dot(rows_ref[:, pl.ds(lanes, half)], slab_ref[...])

    @pl.when(slot > offset)
    def _():
        total_ref[:, half:] += dot_t(rows_ref[:, pl.ds(lanes, tile)], slab_ref[...])

    @pl.when(slot == offset)
    def _():
        low, high = triangles(slab_ref)
        head, tail = own[:, :half], own[:, half:]
        total_ref[:, :half] += dot(head, low)
        total_ref[:, half:] += dot(head, slab_ref[:, half:]) + dot(tail, high)


def all_toward_own(place_ref, slab_ref, rows_ref, own, total_ref, fetches=None):
    slots = rows_ref.shape[1] // own.shape[1]
    half = slab_ref.shape[0] // slots
    for slot in range(slots):
        if fetches is not None:
            fetches[slot].wait()
        toward_own(slot, place_ref[0], slot_of(slab_ref, slot, half), rows_ref, own, total_ref)


def first_own_kernel(
    place_ref, slab_ref, received_ref, base_ref, extra_ref, begun_hbm,
    out_ref, stored_hbm, total_ref, rows_ref, stored
):
    stores = slot_copies(slab_ref, stored_hbm, stored, first=STORED_FIRST)
    for store in stores:
        store.start()
    rhs, tile = base_ref.shape
    slots = rows_ref.shape[1] // tile
    width = tile // LANES
    total_ref[...] = extra_ref[...]
    gather_rows(place_ref, received_ref, rows_ref, tile, slots)
    all_toward_own(place_ref, slab_ref, rows_ref, base_ref[...].astype(BF16), total_ref)
    size = rhs * tile // LANES
    source = place_ref[6]
    planes = received_ref.shape[0] // rhs
    part = slice(slots * width, (slots + 1) * width)
    reduced = received_ref[source, part, :].astype(F32)
    for plane in range(1, planes):
        reduced = reduced + received_ref[plane * rhs + source, part, :].astype(F32)
    reduced = reduced.astype(BF16)
    tiles = to_tiles(total_ref[...]).astype(BF16)
    for copy in range(out_ref.shape[0]):
        out_ref[copy, :size, :] = tiles
        out_ref[copy, size:, :] = reduced
    for store in stores:
        store.wait()


def combine_kernel(place_ref, received_ref, scaled_ref, mid_ref, own_ref, out_ref):
    rhs, tile = scaled_ref.shape
    size = rhs * tile // LANES
    total = received_ref[0, :size, :].astype(F32)
    for sender in range(1, received_ref.shape[0]):
        total = total + received_ref[sender, :size, :].astype(F32)
    others = flat_rows(received_ref[:, size:, :].astype(F32))
    mid = (from_tiles(total, rhs) + others) + scaled_ref[...]
    mid_ref[...] = mid
    own_ref[...] = mid.astype(BF16)
    share = share_of(mid, place_ref[1]).astype(BF16)
    for copy in range(out_ref.shape[0]):
        out_ref[copy, :, :] = share


def three_parts(values):
    first = values.astype(BF16).astype(F32)
    rest = values - first
    second = rest.astype(BF16).astype(F32)
    return first, second, rest - second


def pack_sums(values, used):
    parts = [part[:, :used] for part in three_parts(values)]
    blank = jnp.zeros((values.shape[0], LANES - 3 * used), F32)
    return jnp.concatenate(parts + [blank], axis=1).astype(BF16)


def unpack_sums(values, used):
    return (values[:, :used] + values[:, used : 2 * used]) + values[:, 2 * used : 3 * used]


def pair_kernel(
    place_ref, received_ref, own_ref, extra_ref, sent_ref, grams_ref, out_ref, rows_ref, sums_ref
):
    rhs, tile = own_ref.shape
    slots = sent_ref.shape[0]
    size = rhs * tile // LANES
    gather_rows(place_ref, received_ref, rows_ref, tile, slots)
    pair = dot_t(extra_ref[...].astype(BF16), own_ref[...])
    for part in range(slots):
        pair = pair + dot_t(sent_ref[part], rows_ref[:, part * tile : (part + 1) * tile])
    sums_ref[...] = grams_ref[...]
    sums_ref[:, :rhs] = pair
    packed = pack_sums(sums_ref[...], 5 * rhs)
    for target in range(out_ref.shape[0]):
        out_ref[target, size:, :] = packed
    for part in range(slots):
        tiles = to_tiles(sent_ref[part].astype(F32)).astype(BF16)
        for target in range(part, out_ref.shape[0], slots):
            out_ref[target, :size, :] = tiles


def second_own_kernel(
    place_ref, slab_hbm, rows_ref, own_ref, extra_ref, out_ref, total_ref, slab_ref, arrived
):
    fetches = slot_copies(slab_hbm, slab_ref, arrived)
    for fetch in fetches:
        fetch.start()
    total_ref[...] = extra_ref[...]
    all_toward_own(place_ref, slab_ref, rows_ref, own_ref[...], total_ref, fetches)
    out_ref[...] = to_tiles(total_ref[...])


def summed(received_ref):
    total = received_ref[0, :, :].astype(F32)
    for sender in range(1, received_ref.shape[0]):
        total = total + received_ref[sender, :, :].astype(F32)
    return total


def join_kernel(place_ref, received_ref, own_ref, out_ref):
    size, lanes = own_ref.shape
    rhs = out_ref.shape[1] - size
    total = summed(received_ref)
    packed = pack_sums(unpack_sums(total[size:, :], 5 * rhs), 5 * rhs)
    planes = out_ref.shape[0] // rhs
    for plane in range(planes):
        for_own = place_ref[2] == plane
        for_row = jnp.logical_and(place_ref[5] == plane, place_ref[3] == place_ref[7])
        value = jnp.where(for_own, own_ref[...], 0.0) + jnp.where(for_row, total[:size, :], 0.0)
        value = value.astype(BF16)
        for copy in range(rhs):
            out_ref[plane * rhs + copy, :size, :] = value
            out_ref[plane * rhs + copy, size:, :] = packed


SMEM = pl.BlockSpec(memory_space=pltpu.SMEM)
PARAMS = pltpu.CompilerParams(vmem_limit_bytes=VMEM_LIMIT)


def struct(shape, dtype):
    return jax.ShapeDtypeStruct(shape, dtype)


def in_place(values):
    return pltpu.with_memory_space_constraint(values, pltpu.VMEM)


def in_hbm(values):
    return pltpu.with_memory_space_constraint(values, pltpu.HBM)


def plain(kernel, outs, name, *operands, scalars=True, scratch=(), in_memory=()):
    specs = [pl.BlockSpec(memory_space=pltpu.VMEM)] * len(operands)
    if scalars:
        specs[0] = SMEM
    for index in in_memory:
        specs[index] = pl.BlockSpec(memory_space=pltpu.HBM)
    return pl.pallas_call(
        kernel,
        in_specs=specs,
        out_shape=outs,
        scratch_shapes=scratch,
        compiler_params=PARAMS,
        name=name,
    )(*operands)


def times(left, right):
    total = left[:, 0:1] * right[0:1, :]
    for index in range(1, left.shape[1]):
        total = total + left[:, index : index + 1] * right[index : index + 1, :]
    return total


def inverses(matrices):
    size = matrices[0].shape[0]
    row = lax.broadcasted_iota(jnp.int32, (size, size), 0)
    col = lax.broadcasted_iota(jnp.int32, (size, size), 1)
    eye = jnp.where(row == col, 1.0, 0.0).astype(F32)
    work = [(matrix, eye) for matrix in matrices]
    for step in range(size):
        here = row == step
        following = []
        for left, right in work:
            scale = 1.0 / left[step : step + 1, step : step + 1]
            left_row = left[step : step + 1, :] * scale
            right_row = right[step : step + 1, :] * scale
            column = left[:, step : step + 1]
            following.append(
                (
                    jnp.where(here, left_row, left - column * left_row),
                    jnp.where(here, right_row, right - column * right_row),
                )
            )
        work = following
    return [right for left, right in work], eye


def final_kernel(
    received_ref, base_ref, mid_ref, shifted_ref, solution_ref, residual_ref
):
    rhs, tile = base_ref.shape
    size = rhs * tile // LANES
    total = summed(received_ref)
    gram = unpack_sums(total[size:, :], 5 * rhs)
    half_wy, bb, yb, yy, wy = (gram[:, index * rhs : (index + 1) * rhs] for index in range(5))
    wy = wy + (half_wy + half_wy.T)
    curvature = yb + SHIFT * bb
    (inverse_curvature, inverse_bb), eye = inverses([curvature, bb])
    step_t = times(bb, inverse_curvature)
    step = times(inverse_curvature, bb)
    a1, a1_t = eye - SHIFT * step_t, eye - SHIFT * step
    b1, b1_t = -step_t, -step

    def inner(a, a_t, b, b_t, first, cross, last):
        return times(times(a, first) + times(b, cross), a_t) + times(
            times(a, cross) + times(b, last), b_t
        )

    next_gram = inner(a1, a1_t, b1, b1_t, bb, yb, yy)
    a2 = a1 + times(next_gram, inverse_bb)
    a2_t = a1_t + times(inverse_bb, next_gram)
    curvature = inner(a2, a2_t, b1, b1_t, yb + SHIFT * bb, yy + SHIFT * yb, wy + SHIFT * yy)
    (inverse_curvature,), eye = inverses([curvature])
    last_t = times(next_gram, inverse_curvature)
    base, mid = base_ref[...], mid_ref[...]
    top = from_tiles(total[:size, :], rhs) + shifted_ref[...] * mid
    from_mid = times(last_t, b1)
    from_base = times(last_t, a2)
    solution_ref[...] = times(step_t + from_base, base) + times(from_mid, mid)
    residual_ref[...] = (
        times(a1 - SHIFT * from_base, base)
        + times(b1 - from_base - SHIFT * from_mid, mid)
        - times(from_mid, top)
    )


def local(kernel_codes, tile_scales, kernel_diagonal, noise_variance, targets):
    rhs, tile = targets.shape
    slots = kernel_codes.shape[0] // (tile // 2)
    width = tile // LANES
    size = rhs * width
    row_count = lax.axis_size("row")
    col_count = lax.axis_size("col")
    side = slots * slots
    planes = col_count // side
    row_index = lax.axis_index("row")
    col_index = lax.axis_index("col")
    plane, spot = col_index // side, col_index % side
    place = jnp.stack(
        [
            col_index - row_index * slots,
            row_index,
            plane,
            spot // slots,
            spot,
            row_index // (row_count // planes),
            plane * (row_count // planes) + spot // slots,
            row_index % (row_count // planes),
        ]
    ).astype(jnp.int32)
    near = [[first * side + index for index in range(side)] for first in range(planes)]
    deep = [
        [row * col_count + first * side + index for first in range(planes) for row in range(row_count)]
        for index in range(side)
    ]
    deep_count = planes * row_count

    def exchange_near(values):
        return lax.all_to_all(values, "col", 0, 0, axis_index_groups=near)

    def exchange_deep(values):
        return lax.all_to_all(values, ("row", "col"), 0, 0, axis_index_groups=deep)

    def exchange_row(values):
        return lax.all_to_all(values, "row", 0, 0)

    scales = tile_scales.T
    out_shape = (slots, slots, size + width, LANES)
    in_vmem = pltpu.VMEM(kernel_codes.shape, BF16)
    small = len((scales, targets, kernel_diagonal, noise_variance))
    slabs, stored, outgoing, extra, scaled, shifted = pl.pallas_call(
        first_rows_kernel,
        in_specs=[SMEM] + [pl.BlockSpec(memory_space=pltpu.HBM)] * 5,
        out_specs=[pl.BlockSpec(memory_space=pltpu.VMEM), pl.BlockSpec(memory_space=pltpu.HBM)]
        + [pl.BlockSpec(memory_space=pltpu.VMEM)] * 4,
        out_shape=[in_vmem, pltpu.HBM(kernel_codes.shape, BF16), struct(out_shape, BF16)]
        + [struct((rhs, tile), F32)] * 2
        + [struct((1, tile), F32)],
        scratch_shapes=[
            pltpu.VMEM((tile_scales.shape[0], tile), F32),
            pltpu.VMEM(kernel_codes.shape, BF16),
            pltpu.VMEM(scales.shape, F32),
            pltpu.VMEM(targets.shape, F32),
            pltpu.VMEM((2, tile), F32),
            pltpu.SemaphoreType.DMA((4 * slots,)),
            pltpu.SemaphoreType.DMA((slots,)),
            pltpu.SemaphoreType.DMA((small,)),
        ],
        compiler_params=PARAMS,
        name="first_rows",
    )(
        place,
        in_hbm(kernel_codes),
        in_hbm(scales),
        in_hbm(targets),
        in_hbm(kernel_diagonal),
        in_hbm(noise_variance),
    )
    received = exchange_near(outgoing.reshape(side, size + width, LANES))
    relayed = plain(
        functools.partial(relay_kernel, width),
        struct((deep_count, (slots + 1) * width, LANES), BF16),
        "relay",
        received,
        scalars=False,
    )
    received = exchange_deep(relayed)
    vmem, hbm = pl.BlockSpec(memory_space=pltpu.VMEM), pl.BlockSpec(memory_space=pltpu.HBM)
    message, stored = pl.pallas_call(
        first_own_kernel,
        in_specs=[SMEM] + [vmem] * 4 + [hbm],
        out_specs=[vmem, hbm],
        out_shape=[
            struct((row_count, size + width, LANES), BF16),
            pltpu.HBM(kernel_codes.shape, BF16),
        ],
        scratch_shapes=[
            pltpu.VMEM((rhs, tile), F32),
            pltpu.VMEM((rhs, slots * tile), BF16),
            pltpu.SemaphoreType.DMA((slots,)),
        ],
        input_output_aliases={5: 1},
        compiler_params=PARAMS,
        name="first_own",
    )(place, in_place(slabs), received, targets, extra, in_hbm(stored))
    received = exchange_row(message)
    mid, own, outgoing = plain(
        combine_kernel,
        [struct((rhs, tile), F32), struct((rhs, tile), BF16), struct((side, width, LANES), BF16)],
        "combine",
        place,
        received,
        scaled,
    )
    received = exchange_near(outgoing)
    fetched = [pltpu.VMEM(kernel_codes.shape, BF16), pltpu.SemaphoreType.DMA((slots,))]
    sent, extra, grams = plain(
        functools.partial(second_rows_kernel, row_count),
        [
            struct((slots, rhs, tile), BF16),
            struct((rhs, tile), F32),
            struct((rhs, LANES), F32),
        ],
        "second_rows",
        place,
        in_hbm(stored),
        own,
        targets,
        mid,
        shifted,
        scratch=fetched,
        in_memory=(1,),
    )
    relayed = plain(
        spread_kernel,
        struct((deep_count, slots * width, LANES), BF16),
        "spread",
        received,
        scalars=False,
    )
    received = exchange_deep(relayed)
    outgoing, rows = pl.pallas_call(
        pair_kernel,
        in_specs=[SMEM] + [pl.BlockSpec(memory_space=pltpu.VMEM)] * 5,
        out_shape=[
            struct((side, size + rhs, LANES), BF16),
            struct((rhs, slots * tile), BF16),
        ],
        scratch_shapes=[pltpu.VMEM((rhs, LANES), F32)],
        compiler_params=PARAMS,
        name="pair",
    )(place, received, own, extra, sent, grams)
    received = exchange_near(outgoing)
    total = plain(
        second_own_kernel,
        struct((size, LANES), F32),
        "second_own",
        place,
        in_hbm(stored),
        rows,
        own,
        extra,
        scratch=[pltpu.VMEM((rhs, tile), F32), *fetched],
        in_memory=(1,),
    )
    outgoing = plain(
        join_kernel,
        struct((deep_count, size + rhs, LANES), BF16),
        "join",
        place,
        received,
        total,
    )
    received = exchange_deep(outgoing)
    return tuple(
        plain(
            final_kernel,
            [struct((rhs, tile), F32)] * 2,
            "small_solves",
            received,
            targets,
            mid,
            shifted,
            scalars=False,
        )
    )


def solution(mesh):
    in_specs = (P("row", "col"), P("row", "col"), P("col"), P("col"), P(None, "col"))
    out_specs = (P(None, "col"), P(None, "col"))
    return jax.shard_map(local, mesh=mesh, in_specs=in_specs, out_specs=out_specs, check_vma=False)
```

```python
import functools

import jax
import jax.numpy as jnp
from jax import lax
from jax.experimental import pallas as pl
from jax.experimental.pallas import tpu as pltpu
from jax.sharding import PartitionSpec as P

F32 = jnp.float32
BF16 = jnp.bfloat16
SHIFT = 3.0
STORED_FIRST = 2
VMEM_LIMIT = 32 * 1024 * 1024


def spread_scales(scales_ref, wide_ref):
    col_blocks = scales_ref.shape[0]
    cols = wide_ref.shape[1]
    lane_block = lax.broadcasted_iota(jnp.int32, (col_blocks, cols), 1) // (cols // col_blocks)
    own_block = lax.broadcasted_iota(jnp.int32, (col_blocks, cols), 0)
    spread = jnp.where(lane_block == own_block, 1.0, 0.0).astype(BF16)
    parts = jnp.concatenate(three_parts(scales_ref[...]), axis=1).astype(BF16)
    wide = lax.dot_general(
        parts, spread, (((0,), (0,)), ((), ())), preferred_element_type=F32
    )
    count = wide_ref.shape[0]
    wide_ref[...] = wide[:count] + (wide[count : 2 * count] + wide[2 * count :])


def dequantize_slot(slot, slots, codes_ref, wide_ref, slab_ref, copies=()):
    rows = codes_ref.shape[0] // slots
    block_rows = wide_ref.shape[0] // slots
    order = rows // block_rows
    for index, block in enumerate(range(slot * block_rows, (slot + 1) * block_rows)):
        if copies and index % (block_rows // len(copies)) == 0:
            copies[index // (block_rows // len(copies))].wait()
        part = slice(block * order, (block + 1) * order)
        wide = wide_ref[block : block + 1, :]
        slab_ref[part, :] = (codes_ref[part, :].astype(F32) * wide).astype(BF16)


NT = (((1,), (1,)), ((), ()))


def dot(left, right):
    return jnp.dot(left, right, preferred_element_type=F32)


def dot_t(left, right):
    return lax.dot_general(left, right, NT, preferred_element_type=F32)


def triangles(slab_ref):
    half = slab_ref.shape[0]
    mixed = slab_ref[:, :half]
    row = lax.broadcasted_iota(jnp.int32, (half, half), 0)
    col = lax.broadcasted_iota(jnp.int32, (half, half), 1)
    zero = jnp.zeros_like(mixed)
    return jnp.where(row > col, mixed, zero), jnp.where(row < col, mixed, zero)


LANES = 128


def to_tiles(values):
    count = values.shape[1] // LANES
    return jnp.concatenate(
        [values[:, part * LANES : (part + 1) * LANES] for part in range(count)], axis=0
    )


def from_tiles(tiles, rhs):
    count = tiles.shape[0] // rhs
    return jnp.concatenate(
        [tiles[part * rhs : (part + 1) * rhs, :] for part in range(count)], axis=1
    )


def row_tiles(values):
    return values.reshape(values.shape[0], values.shape[1] // LANES, LANES)


def flat_rows(tiles):
    return tiles.reshape(tiles.shape[0], tiles.shape[1] * LANES)


def share_of(values, row_index):
    tiles = row_tiles(values)
    row = lax.broadcasted_iota(jnp.int32, tiles.shape, 0)
    return jnp.sum(jnp.where(row == row_index, tiles, 0.0), axis=0)


def toward_rows(slot, offset, slab_ref, own, put, extra_ref, beside):
    half, tile = slab_ref.shape
    rhs = own.shape[0]

    @pl.when(slot < offset)
    def _():
        beside()
        second = dot_t(own, slab_ref[...])
        put(jnp.concatenate([second, jnp.zeros((rhs, tile - half), F32)], axis=1))

    @pl.when(slot > offset)
    def _():
        beside()
        first = dot(own[:, half:], slab_ref[...])
        put(first)

    @pl.when(slot == offset)
    def _():
        beside()
        low, high = triangles(slab_ref)
        head, tail = own[:, :half], own[:, half:]
        extra_ref[:, :half] = dot_t(head, low) + dot_t(tail, slab_ref[:, half:])
        extra_ref[:, half:] = dot_t(tail, high)
        put(jnp.zeros((rhs, tile), F32))


def slot_copies(source_ref, target_ref, semaphores, first=0, last=None):
    slots = semaphores.shape[0]
    half = source_ref.shape[0] // slots
    copies = []
    for slot in range(first, slots if last is None else last):
        part = pl.ds(slot * half, half)
        copies.append(
            pltpu.make_async_copy(
                source_ref.at[part, :], target_ref.at[part, :], semaphores.at[slot]
            )
        )
    return copies


def slot_of(slab_ref, slot, half):
    return slab_ref.at[pl.ds(slot * half, half), :]


def first_rows_kernel(
    place_ref,
    codes_hbm,
    scales_hbm,
    base_hbm,
    diagonal_hbm,
    noise_hbm,
    slab_ref,
    stored_hbm,
    out_ref,
    extra_ref,
    scaled_ref,
    shifted_ref,
    wide_ref,
    codes_ref,
    scales_ref,
    base_ref,
    points_ref,
    arrived,
    stored,
    small,
):
    slots = out_ref.shape[1]
    half = slab_ref.shape[0] // slots
    sources = (scales_hbm, base_hbm, diagonal_hbm, noise_hbm)
    targets = (scales_ref, base_ref, points_ref.at[0], points_ref.at[1])
    inputs = [
        pltpu.make_async_copy(source, target, small.at[index])
        for index, (source, target) in enumerate(zip(sources, targets))
    ]
    copies = slot_copies(codes_hbm, codes_ref, arrived)
    stores = slot_copies(slab_ref, stored_hbm, stored, last=STORED_FIRST)
    each = len(copies) // slots
    for copy in inputs[:1] + copies[:each] + inputs[1:] + copies[each:]:
        copy.start()
    rhs, tile = base_ref.shape
    size = rhs * tile // LANES
    inputs[0].wait()
    spread_scales(scales_ref, wide_ref)
    extra_ref[...] = jnp.zeros_like(extra_ref)
    dequantize_slot(0, slots, codes_ref, wide_ref, slab_ref, copies[:each])
    stores[0].start()
    inputs[1].wait()
    own = base_ref[...].astype(BF16)
    for slot in range(slots):
        for copy in copies[(slot + 1) * each : (slot + 2) * each]:
            copy.wait()

        def beside(slot=slot):
            if slot + 1 < slots:
                dequantize_slot(slot + 1, slots, codes_ref, wide_ref, slab_ref)

        def put(values, slot=slot):
            tiles = to_tiles(values).astype(BF16)
            for copy in range(slots):
                out_ref[copy, slot, :size, :] = tiles

        view = slot_of(slab_ref, slot, half)
        toward_rows(slot, place_ref[0], view, own, put, extra_ref, beside)
        if slot + 1 < len(stores):
            stores[slot + 1].start()
    for copy in inputs[2:]:
        copy.wait()
    base = base_ref[...]
    shifted = points_ref[0:1, :].astype(BF16).astype(F32) + (points_ref[1:2, :] - SHIFT)
    shifted_ref[...] = shifted
    scaled_ref[...] = shifted * base
    share = share_of(base, place_ref[1]).astype(BF16)
    for copy in range(slots):
        for slot in range(slots):
            out_ref[copy, slot, size:, :] = share
    for store in stores:
        store.wait()


def second_rows_kernel(
    copies, place_ref, slab_hbm, own_ref, base_ref, mid_ref, shifted_ref,
    out_ref, extra_ref, sums_ref, slab_ref, arrived
):
    fetches = slot_copies(slab_hbm, slab_ref, arrived)
    for fetch in fetches:
        fetch.start()
    rhs = own_ref.shape[0]
    base, mid = base_ref[...], mid_ref[...]
    exact = functools.partial(
        lax.dot_general,
        dimension_numbers=NT,
        precision=lax.Precision.HIGHEST,
        preferred_element_type=F32,
    )
    on_base = exact(jnp.concatenate([base, mid]), base)
    on_mid = exact(jnp.concatenate([mid, shifted_ref[...] * mid]), mid)
    sums_ref[...] = jnp.zeros_like(sums_ref)
    for part, value in enumerate((on_base[:rhs], on_base[rhs:], on_mid[:rhs], on_mid[rhs:])):
        sums_ref[:, (part + 1) * rhs : (part + 2) * rhs] = value * (1.0 / copies)
    extra_ref[...] = jnp.zeros_like(extra_ref)
    for slot in range(out_ref.shape[0]):

        def put(values, slot=slot):
            out_ref[slot, :, :] = values.astype(BF16)

        half = slab_ref.shape[0] // out_ref.shape[0]
        view = slot_of(slab_ref, slot, half)
        fetches[slot].wait()
        toward_rows(slot, place_ref[0], view, own_ref[...], put, extra_ref, lambda: None)


def relay_kernel(width, received_ref, out_ref):
    senders, height, lanes = received_ref.shape
    copies, full, lanes = out_ref.shape
    size = height - width
    slots = full // width - 1
    rhs = size // width
    reduced = received_ref[0, :size, :].astype(F32)
    for sender in range(1, senders):
        reduced = reduced + received_ref[sender, :size, :].astype(F32)
    rows = row_tiles(from_tiles(reduced, rhs)).astype(BF16)
    groups = []
    for first in range(0, senders, slots):
        pieces = [received_ref[first + part, size:, :].astype(F32) for part in range(slots)]
        groups.append(jnp.concatenate(pieces, axis=0).astype(BF16))
    for copy in range(copies):
        out_ref[copy, : slots * width, :] = groups[copy % len(groups)]
        out_ref[copy, slots * width :, :] = rows[copy % rhs]


def spread_kernel(received_ref, out_ref):
    senders, width, lanes = received_ref.shape
    slots = out_ref.shape[1] // width
    for first in range(0, senders, slots):
        pieces = [received_ref[first + part].astype(F32) for part in range(slots)]
        group = jnp.concatenate(pieces, axis=0).astype(BF16)
        for copy in range(first // slots, out_ref.shape[0], senders // slots):
            out_ref[copy, :, :] = group


def gather_rows(place_ref, received_ref, rows_ref, tile, slots):
    rhs = rows_ref.shape[0]
    start = place_ref[5] * rhs
    size = slots * tile // LANES
    piece = received_ref[pl.ds(start, rhs), :size, :].astype(F32)
    rows_ref[...] = flat_rows(piece).astype(BF16)


def toward_own(slot, offset, slab_ref, rows_ref, own, total_ref):
    half, tile = slab_ref.shape
    lanes = pl.multiple_of(slot * tile, tile)

    @pl.when(slot < offset)
    def _():
        total_ref[...] += dot(rows_ref[:, pl.ds(lanes, half)], slab_ref[...])

    @pl.when(slot > offset)
    def _():
        total_ref[:, half:] += dot_t(rows_ref[:, pl.ds(lanes, tile)], slab_ref[...])

    @pl.when(slot == offset)
    def _():
        low, high = triangles(slab_ref)
        head, tail = own[:, :half], own[:, half:]
        total_ref[:, :half] += dot(head, low)
        total_ref[:, half:] += dot(head, slab_ref[:, half:]) + dot(tail, high)


def all_toward_own(place_ref, slab_ref, rows_ref, own, total_ref, fetches=None):
    slots = rows_ref.shape[1] // own.shape[1]
    half = slab_ref.shape[0] // slots
    for slot in range(slots):
        if fetches is not None:
            fetches[slot].wait()
        toward_own(slot, place_ref[0], slot_of(slab_ref, slot, half), rows_ref, own, total_ref)


def first_own_kernel(
    place_ref, slab_ref, received_ref, base_ref, extra_ref, begun_hbm,
    out_ref, stored_hbm, total_ref, rows_ref, stored
):
    stores = slot_copies(slab_ref, stored_hbm, stored, first=STORED_FIRST)
    for store in stores:
        store.start()
    rhs, tile = base_ref.shape
    slots = rows_ref.shape[1] // tile
    width = tile // LANES
    total_ref[...] = extra_ref[...]
    gather_rows(place_ref, received_ref, rows_ref, tile, slots)
    all_toward_own(place_ref, slab_ref, rows_ref, base_ref[...].astype(BF16), total_ref)
    size = rhs * tile // LANES
    source = place_ref[6]
    planes = received_ref.shape[0] // rhs
    part = slice(slots * width, (slots + 1) * width)
    reduced = received_ref[source, part, :].astype(F32)
    for plane in range(1, planes):
        reduced = reduced + received_ref[plane * rhs + source, part, :].astype(F32)
    reduced = reduced.astype(BF16)
    tiles = to_tiles(total_ref[...]).astype(BF16)
    for copy in range(out_ref.shape[0]):
        out_ref[copy, :size, :] = tiles
        out_ref[copy, size:, :] = reduced
    for store in stores:
        store.wait()


def combine_kernel(place_ref, received_ref, scaled_ref, mid_ref, own_ref, out_ref):
    rhs, tile = scaled_ref.shape
    size = rhs * tile // LANES
    total = received_ref[0, :size, :].astype(F32)
    for sender in range(1, received_ref.shape[0]):
        total = total + received_ref[sender, :size, :].astype(F32)
    others = flat_rows(received_ref[:, size:, :].astype(F32))
    mid = (from_tiles(total, rhs) + others) + scaled_ref[...]
    mid_ref[...] = mid
    own_ref[...] = mid.astype(BF16)
    share = share_of(mid, place_ref[1]).astype(BF16)
    for copy in range(out_ref.shape[0]):
        out_ref[copy, :, :] = share


def three_parts(values):
    first = values.astype(BF16).astype(F32)
    rest = values - first
    second = rest.astype(BF16).astype(F32)
    return first, second, rest - second


def pack_sums(values, used):
    parts = [part[:, :used] for part in three_parts(values)]
    blank = jnp.zeros((values.shape[0], LANES - 3 * used), F32)
    return jnp.concatenate(parts + [blank], axis=1).astype(BF16)


def unpack_sums(values, used):
    return (values[:, :used] + values[:, used : 2 * used]) + values[:, 2 * used : 3 * used]


def pair_kernel(
    place_ref, received_ref, own_ref, extra_ref, sent_ref, grams_ref, out_ref, rows_ref, sums_ref
):
    rhs, tile = own_ref.shape
    slots = sent_ref.shape[0]
    size = rhs * tile // LANES
    gather_rows(place_ref, received_ref, rows_ref, tile, slots)
    pair = dot_t(extra_ref[...].astype(BF16), own_ref[...])
    for part in range(slots):
        pair = pair + dot_t(sent_ref[part], rows_ref[:, part * tile : (part + 1) * tile])
    sums_ref[...] = grams_ref[...]
    sums_ref[:, :rhs] = pair
    packed = pack_sums(sums_ref[...], 5 * rhs)
    for target in range(out_ref.shape[0]):
        out_ref[target, size:, :] = packed
    for part in range(slots):
        tiles = to_tiles(sent_ref[part].astype(F32)).astype(BF16)
        for target in range(part, out_ref.shape[0], slots):
            out_ref[target, :size, :] = tiles


def second_own_kernel(
    place_ref, slab_hbm, rows_ref, own_ref, extra_ref, out_ref, total_ref, slab_ref, arrived
):
    fetches = slot_copies(slab_hbm, slab_ref, arrived)
    for fetch in fetches:
        fetch.start()
    total_ref[...] = extra_ref[...]
    all_toward_own(place_ref, slab_ref, rows_ref, own_ref[...], total_ref, fetches)
    out_ref[...] = to_tiles(total_ref[...])


def summed(received_ref):
    total = received_ref[0, :, :].astype(F32)
    for sender in range(1, received_ref.shape[0]):
        total = total + received_ref[sender, :, :].astype(F32)
    return total


def join_kernel(place_ref, received_ref, own_ref, out_ref):
    size, lanes = own_ref.shape
    rhs = out_ref.shape[1] - size
    total = summed(received_ref)
    packed = pack_sums(unpack_sums(total[size:, :], 5 * rhs), 5 * rhs)
    planes = out_ref.shape[0] // rhs
    for plane in range(planes):
        for_own = place_ref[2] == plane
        for_row = jnp.logical_and(place_ref[5] == plane, place_ref[3] == place_ref[7])
        value = jnp.where(for_own, own_ref[...], 0.0) + jnp.where(for_row, total[:size, :], 0.0)
        value = value.astype(BF16)
        for copy in range(rhs):
            out_ref[plane * rhs + copy, :size, :] = value
            out_ref[plane * rhs + copy, size:, :] = packed


SMEM = pl.BlockSpec(memory_space=pltpu.SMEM)
PARAMS = pltpu.CompilerParams(vmem_limit_bytes=VMEM_LIMIT)


def struct(shape, dtype):
    return jax.ShapeDtypeStruct(shape, dtype)


def in_place(values):
    return pltpu.with_memory_space_constraint(values, pltpu.VMEM)


def in_hbm(values):
    return pltpu.with_memory_space_constraint(values, pltpu.HBM)


def plain(kernel, outs, name, *operands, scalars=True, scratch=(), in_memory=()):
    specs = [pl.BlockSpec(memory_space=pltpu.VMEM)] * len(operands)
    if scalars:
        specs[0] = SMEM
    for index in in_memory:
        specs[index] = pl.BlockSpec(memory_space=pltpu.HBM)
    return pl.pallas_call(
        kernel,
        in_specs=specs,
        out_shape=outs,
        scratch_shapes=scratch,
        compiler_params=PARAMS,
        name=name,
    )(*operands)


def times(left, right):
    total = left[:, 0:1] * right[0:1, :]
    for index in range(1, left.shape[1]):
        total = total + left[:, index : index + 1] * right[index : index + 1, :]
    return total


def inverses(matrices):
    size = matrices[0].shape[0]
    row = lax.broadcasted_iota(jnp.int32, (size, size), 0)
    col = lax.broadcasted_iota(jnp.int32, (size, size), 1)
    eye = jnp.where(row == col, 1.0, 0.0).astype(F32)
    work = [(matrix, eye) for matrix in matrices]
    for step in range(size):
        here = row == step
        following = []
        for left, right in work:
            scale = 1.0 / left[step : step + 1, step : step + 1]
            left_row = left[step : step + 1, :] * scale
            right_row = right[step : step + 1, :] * scale
            column = left[:, step : step + 1]
            following.append(
                (
                    jnp.where(here, left_row, left - column * left_row),
                    jnp.where(here, right_row, right - column * right_row),
                )
            )
        work = following
    return [right for left, right in work], eye


def final_kernel(
    received_ref, base_ref, mid_ref, shifted_ref, solution_ref, residual_ref
):
    rhs, tile = base_ref.shape
    size = rhs * tile // LANES
    total = summed(received_ref)
    gram = unpack_sums(total[size:, :], 5 * rhs)
    half_wy, bb, yb, yy, wy = (gram[:, index * rhs : (index + 1) * rhs] for index in range(5))
    wy = wy + (half_wy + half_wy.T)
    curvature = yb + SHIFT * bb
    (inverse_curvature, inverse_bb), eye = inverses([curvature, bb])
    step_t = times(bb, inverse_curvature)
    step = times(inverse_curvature, bb)
    a1, a1_t = eye - SHIFT * step_t, eye - SHIFT * step
    b1, b1_t = -step_t, -step

    def inner(a, a_t, b, b_t, first, cross, last):
        return times(times(a, first) + times(b, cross), a_t) + times(
            times(a, cross) + times(b, last), b_t
        )

    next_gram = inner(a1, a1_t, b1, b1_t, bb, yb, yy)
    a2 = a1 + times(next_gram, inverse_bb)
    a2_t = a1_t + times(inverse_bb, next_gram)
    curvature = inner(a2, a2_t, b1, b1_t, yb + SHIFT * bb, yy + SHIFT * yb, wy + SHIFT * yy)
    (inverse_curvature,), eye = inverses([curvature])
    last_t = times(next_gram, inverse_curvature)
    base, mid = base_ref[...], mid_ref[...]
    top = from_tiles(total[:size, :], rhs) + shifted_ref[...] * mid
    from_mid = times(last_t, b1)
    from_base = times(last_t, a2)
    solution_ref[...] = times(step_t + from_base, base) + times(from_mid, mid)
    residual_ref[...] = (
        times(a1 - SHIFT * from_base, base)
        + times(b1 - from_base - SHIFT * from_mid, mid)
        - times(from_mid, top)
    )


def local(kernel_codes, tile_scales, kernel_diagonal, noise_variance, targets):
    rhs, tile = targets.shape
    slots = kernel_codes.shape[0] // (tile // 2)
    width = tile // LANES
    size = rhs * width
    row_count = lax.axis_size("row")
    col_count = lax.axis_size("col")
    side = slots * slots
    planes = col_count // side
    row_index = lax.axis_index("row")
    col_index = lax.axis_index("col")
    plane, spot = col_index // side, col_index % side
    place = jnp.stack(
        [
            col_index - row_index * slots,
            row_index,
            plane,
            spot // slots,
            spot,
            row_index // (row_count // planes),
            plane * (row_count // planes) + spot // slots,
            row_index % (row_count // planes),
        ]
    ).astype(jnp.int32)
    near = [[first * side + index for index in range(side)] for first in range(planes)]
    deep = [
        [row * col_count + first * side + index for first in range(planes) for row in range(row_count)]
        for index in range(side)
    ]
    deep_count = planes * row_count

    def exchange_near(values):
        return lax.all_to_all(values, "col", 0, 0, axis_index_groups=near)

    def exchange_deep(values):
        return lax.all_to_all(values, ("row", "col"), 0, 0, axis_index_groups=deep)

    def exchange_row(values):
        return lax.all_to_all(values, "row", 0, 0)

    scales = tile_scales.T
    out_shape = (slots, slots, size + width, LANES)
    in_vmem = pltpu.VMEM(kernel_codes.shape, BF16)
    small = len((scales, targets, kernel_diagonal, noise_variance))
    slabs, stored, outgoing, extra, scaled, shifted = pl.pallas_call(
        first_rows_kernel,
        in_specs=[SMEM] + [pl.BlockSpec(memory_space=pltpu.HBM)] * 5,
        out_specs=[pl.BlockSpec(memory_space=pltpu.VMEM), pl.BlockSpec(memory_space=pltpu.HBM)]
        + [pl.BlockSpec(memory_space=pltpu.VMEM)] * 4,
        out_shape=[in_vmem, pltpu.HBM(kernel_codes.shape, BF16), struct(out_shape, BF16)]
        + [struct((rhs, tile), F32)] * 2
        + [struct((1, tile), F32)],
        scratch_shapes=[
            pltpu.VMEM((tile_scales.shape[0], tile), F32),
            pltpu.VMEM(kernel_codes.shape, BF16),
            pltpu.VMEM(scales.shape, F32),
            pltpu.VMEM(targets.shape, F32),
            pltpu.VMEM((2, tile), F32),
            pltpu.SemaphoreType.DMA((4 * slots,)),
            pltpu.SemaphoreType.DMA((slots,)),
            pltpu.SemaphoreType.DMA((small,)),
        ],
        compiler_params=PARAMS,
        name="first_rows",
    )(
        place,
        in_hbm(kernel_codes),
        in_hbm(scales),
        in_hbm(targets),
        in_hbm(kernel_diagonal),
        in_hbm(noise_variance),
    )
    received = exchange_near(outgoing.reshape(side, size + width, LANES))
    relayed = plain(
        functools.partial(relay_kernel, width),
        struct((deep_count, (slots + 1) * width, LANES), BF16),
        "relay",
        received,
        scalars=False,
    )
    received = exchange_deep(relayed)
    vmem, hbm = pl.BlockSpec(memory_space=pltpu.VMEM), pl.BlockSpec(memory_space=pltpu.HBM)
    message, stored = pl.pallas_call(
        first_own_kernel,
        in_specs=[SMEM] + [vmem] * 4 + [hbm],
        out_specs=[vmem, hbm],
        out_shape=[
            struct((row_count, size + width, LANES), BF16),
            pltpu.HBM(kernel_codes.shape, BF16),
        ],
        scratch_shapes=[
            pltpu.VMEM((rhs, tile), F32),
            pltpu.VMEM((rhs, slots * tile), BF16),
            pltpu.SemaphoreType.DMA((slots,)),
        ],
        input_output_aliases={5: 1},
        compiler_params=PARAMS,
        name="first_own",
    )(place, in_place(slabs), received, targets, extra, in_hbm(stored))
    received = exchange_row(message)
    mid, own, outgoing = plain(
        combine_kernel,
        [struct((rhs, tile), F32), struct((rhs, tile), BF16), struct((side, width, LANES), BF16)],
        "combine",
        place,
        received,
        scaled,
    )
    received = exchange_near(outgoing)
    fetched = [pltpu.VMEM(kernel_codes.shape, BF16), pltpu.SemaphoreType.DMA((slots,))]
    sent, extra, grams = plain(
        functools.partial(second_rows_kernel, row_count),
        [
            struct((slots, rhs, tile), BF16),
            struct((rhs, tile), F32),
            struct((rhs, LANES), F32),
        ],
        "second_rows",
        place,
        in_hbm(stored),
        own,
        targets,
        mid,
        shifted,
        scratch=fetched,
        in_memory=(1,),
    )
    relayed = plain(
        spread_kernel,
        struct((deep_count, slots * width, LANES), BF16),
        "spread",
        received,
        scalars=False,
    )
    received = exchange_deep(relayed)
    outgoing, rows = pl.pallas_call(
        pair_kernel,
        in_specs=[SMEM] + [pl.BlockSpec(memory_space=pltpu.VMEM)] * 5,
        out_shape=[
            struct((side, size + rhs, LANES), BF16),
            struct((rhs, slots * tile), BF16),
        ],
        scratch_shapes=[pltpu.VMEM((rhs, LANES), F32)],
        compiler_params=PARAMS,
        name="pair",
    )(place, received, own, extra, sent, grams)
    received = exchange_near(outgoing)
    total = plain(
        second_own_kernel,
        struct((size, LANES), F32),
        "second_own",
        place,
        in_hbm(stored),
        rows,
        own,
        extra,
        scratch=[pltpu.VMEM((rhs, tile), F32), *fetched],
        in_memory=(1,),
    )
    outgoing = plain(
        join_kernel,
        struct((deep_count, size + rhs, LANES), BF16),
        "join",
        place,
        received,
        total,
    )
    received = exchange_deep(outgoing)
    return tuple(
        plain(
            final_kernel,
            [struct((rhs, tile), F32)] * 2,
            "small_solves",
            received,
            targets,
            mid,
            shifted,
            scalars=False,
        )
    )


def solution(mesh):
    in_specs = (P("row", "col"), P("row", "col"), P("col"), P("col"), P(None, "col"))
    out_specs = (P(None, "col"), P(None, "col"))
    return jax.shard_map(local, mesh=mesh, in_specs=in_specs, out_specs=out_specs, check_vma=False)
```
